256 devices in a mesh: row: 16 (over x, y_lo, core), col: 16 (over y_hi, z).
Axes of the slice: x: 4, y: 4 (y_hi: 2, y_lo: 2; y = y_hi * 2 + y_lo), z: 8, core: 2. Of those that a mesh axis runs over, the one named last changes fastest.
Arguments:
- design: bfloat16 [12288, 32768], P('row', 'col'), may hold values from -6 to 6
- species: int32 [12288], P('row'), may hold values from 0 to 9
- species_weight: float32 [10], replicated, may hold values from 0.2 to 5
Outputs:
- gram_tiles: float32 [32768, 2048], P(('col', 'row'))
The draws below stay inside these ranges and needn't reach their ends.
All inputs are finite; a program needn't handle non-finite values.
Results may differ from the reference program's by a relative error of at most 0.0029.
Values may be sent and summed in bfloat16 or wider, within the bound.
A program may use at most 64 MiB of HBM per device.

```python
import math
import jax
import jax.numpy as jnp
from jax import lax

BW = 2048
NSPEC = 10
ROWS = 12288
K = 32768
N_COL = 16


def touch_ends(drawn, own_key, least, largest):
    spot = [jax.random.randint(jax.random.fold_in(own_key, axis), (), 0, length) for axis, length in enumerate(drawn.shape)]
    widest = drawn.shape.index(max(drawn.shape))
    next_to = spot[:widest] + [(spot[widest] + 1) % drawn.shape[widest]] + spot[widest + 1:]
    return drawn.at[tuple(spot)].set(least).at[tuple(next_to)].set(largest)


def steps_of(stream_key, extent, cuts, smallest, high):
    level = 1.0
    for axis_at, shards_of in cuts:
        draws = jax.random.uniform(jax.random.fold_in(jax.random.fold_in(stream_key, 6), axis_at), (shards_of,), jnp.float32, smallest / len(cuts), high / len(cuts))
        level = level * jnp.repeat(jnp.exp(draws), extent[axis_at] // shards_of).reshape((-1,) + (1,) * (len(extent) - 1 - axis_at))
    return level


def scatter_about(rng, shape, spread, bound, shards=(), held_as=jnp.bfloat16):
    array = spread * jax.random.normal(rng, shape, jnp.float32)
    if shards:
        array = array * steps_of(rng, shape, shards, -0.22, 0.18)
    return jnp.clip(array, -bound, bound).astype(held_as)


def setup_inputs(seed: int = 0) -> dict:
    key_list = jax.random.split(jax.random.key(seed), 4)
    return {
        "design": scatter_about(key_list[0], (ROWS, K), 1.0, 6.0, ((0, 16), (1, 16))),
        "species": touch_ends(jax.random.randint(key_list[1], (ROWS,), 0, NSPEC), jax.random.fold_in(key_list[1], 1), 0, NSPEC - 1).astype(jnp.int32),
        "species_weight": jnp.clip(jnp.exp(jax.random.uniform(key_list[2], (NSPEC,), jnp.float32, math.log(0.2), math.log(5.0))), 0.2, 5.0),
    }


def reference(design, species, species_weight):
    onehot = (species[:, None] == jnp.arange(NSPEC, dtype=jnp.int32)[None, :]).astype(jnp.float32)
    row_weight = jnp.sum(onehot * species_weight[None, :].astype(jnp.float32), axis=1)
    scaled = (design.astype(jnp.float32) * row_weight[:, None]).astype(jnp.bfloat16)
    normalizer = float(ROWS) ** -0.5

    def one_tile(block):
        left_block = lax.dynamic_slice_in_dim(scaled, (block * BW).astype(jnp.int32), BW, 1)
        right_block = lax.dynamic_slice_in_dim(design, ((N_COL - 1 - block) * BW).astype(jnp.int32), BW, 1)
        product = lax.dot_general(left_block, right_block, (((0,), (0,)), ((), ())), preferred_element_type=jnp.float32)
        return product * normalizer

    stacked = lax.map(one_tile, jnp.arange(N_COL, dtype=jnp.int32))
    return stacked.reshape(N_COL * BW, BW)
```

```python
import jax
import jax.numpy as jnp
from jax import lax
from jax.experimental import pallas as pl
from jax.experimental.pallas import tpu as pltpu
from jax.sharding import PartitionSpec as P

MESH = pl.DeviceIdType.MESH
BF = jnp.bfloat16
F32 = jnp.float32
DEPTH = 768
WIDTH = 2048
NB = 8
NORM = float(12288) ** -0.5


def kernel(
    design, weight, out,
    raw, wv, hi, lo, rbuf, rt, send_a, recv_a, own, send_b, recv_b, half, ret, tile,
    local_sem, ls, lr, ws, wr, rs, rr, as_, ar, bs, br, ts, tr, os_, orr,
):
    row = lax.axis_index("row")
    col = lax.axis_index("col")
    mirror = 15 - col
    core = lax.rem(row, 2)
    chip = lax.div(row, 2)
    y = lax.rem(chip, 2)
    x = lax.div(chip, 2)
    sibling = row + 1 - 2 * core
    across = row + 2 - 4 * y
    computes = lax.rem(col, 2) == 1
    barrier = pltpu.get_barrier_semaphore()

    def copy(src, dst, ss, rs_, to_row, to_col):
        return pltpu.make_async_remote_copy(
            src_ref=src, dst_ref=dst, send_sem=ss, recv_sem=rs_, device_id=(to_row, to_col), device_id_type=MESH
        )

    def greet(to_row, to_col):
        pl.semaphore_signal(barrier, inc=1, device_id=(to_row, to_col), device_id_type=MESH)

    def row_at(j):
        return lax.rem(x + j, 4) * 4 + y * 2 + core

    def design_copy(k, c):
        return copy(
            design.at[:, pl.ds(pl.multiple_of(k * 256 + c * 128, 128), 128)],
            rbuf.at[k, pl.ds(pl.multiple_of(core * DEPTH, DEPTH), DEPTH), :],
            rs.at[k, c], rr.at[k, core], chip * 2 + c, mirror,
        )

    def return_copy(k):
        return copy(
            ret.at[k], out.at[:, pl.ds(pl.multiple_of(chip * 256, 256), 256)], os_.at[k], orr.at[chip], 2 * k + core, mirror
        )

    @pl.when(jnp.logical_not(computes))
    def _():
        for q in range(8):
            greet(2 * q + core, mirror)
        pl.semaphore_wait(barrier, 2)

        def step(k, carry):
            for c in range(2):
                design_copy(k, c).start()

            @pl.when(k >= 2)
            def _():
                for c in range(2):
                    design_copy(k - 2, c).wait_send()

            return carry

        lax.fori_loop(0, NB, step, 0)
        for k in (NB - 2, NB - 1):
            for c in range(2):
                design_copy(k, c).wait_send()
        for q in range(8):
            copy(
                ret.at[0], out.at[:, pl.ds(q * 256, 256)], os_.at[0], orr.at[q], row, mirror
            ).wait_recv()

    @pl.when(computes)
    def _():
        greet(chip * 2, mirror)
        greet(chip * 2 + 1, mirror)
        greet(sibling, col)
        greet(across, col)
        for j in range(1, 4):
            greet(row_at(j), col)
        mine = pltpu.make_async_copy(design, raw.at[core], local_sem.at[0])
        mine_w = pltpu.make_async_copy(weight, wv.at[core], local_sem.at[1])
        mine.start()
        mine_w.start()
        pl.semaphore_wait(barrier, 13)
        theirs = copy(design, raw.at[core], ls, lr, sibling, col)
        theirs_w = copy(weight, wv.at[core], ws, wr, sibling, col)
        theirs_w.start()
        theirs.start()

        def scale(s):
            def piece(i, carry):
                at = pl.ds(pl.multiple_of(i * 32, 32), 32)
                to = pl.ds(pl.multiple_of(s * DEPTH + i * 32, 32), 32)
                value = raw[s, at, :].astype(F32) * wv[s, at, 0:1]
                high = value.astype(BF)
                hi[to, :] = high
                lo[to, :] = (value - high.astype(F32)).astype(BF)
                return carry

            lax.fori_loop(0, DEPTH // 32, piece, 0)

        mine.wait()
        mine_w.wait()
        scale(core)
        theirs_w.wait()
        theirs.wait()
        scale(1 - core)

        def copy_a(k, j):
            return copy(send_a.at[k, j - 1], recv_a.at[k, j - 1], as_.at[k, j - 1], ar.at[k, j - 1], row_at(j), col)

        def copy_b(k):
            return copy(send_b.at[k], recv_b.at[k], bs.at[k], br.at[k], across, col)

        def copy_t(k):
            return copy(
                tile.at[k], out.at[:, pl.ds(pl.multiple_of(k * 256 + core * 128, 128), 128)], ts.at[k], tr.at[k], sibling, col
            )

        def multiply(k):
            for c in range(2):
                copy(
                    design.at[:, pl.ds(0, 128)], rbuf.at[k, pl.ds(c * DEPTH, DEPTH), :], rs.at[k, c], rr.at[k, c], row, mirror
                ).wait_recv()
            rt[...] = rbuf[k].T
            for j in (2, 1, 3, 0):
                at = pl.ds(pl.multiple_of(lax.rem(x + j, 4) * 512, 512), 512)
                part = jnp.dot(rt[...], hi[:, at], preferred_element_type=F32)
                part += jnp.dot(rt[...], lo[:, at], preferred_element_type=F32)
                if j:
                    send_a[k, j - 1] = part.astype(BF)
                    copy_a(k, j).start()
                else:
                    own[k] = part

        def sum_x(k):
            for j in range(1, 4):
                copy_a(k, j).wait_recv()
            at_mine = pl.ds(pl.multiple_of(y * 256, 256), 256)
            at_other = pl.ds(pl.multiple_of(256 - y * 256, 256), 256)

            def total(at):
                t = own[k, :, at]
                for j in range(3):
                    t += recv_a[k, j, :, at].astype(F32)
                return t

            send_b[k] = total(at_other)
            copy_b(k).start()
            half[k] = total(at_mine)

        def sum_y(k):
            copy_b(k).wait_recv()
            ret[k] = (half[k] + recv_b[k]) * NORM
            return_copy(k).start()
            tile[k] = ret[k, :, pl.ds(pl.multiple_of(128 - core * 128, 128), 128)].T
            copy_t(k).start()
            out[:, pl.ds(pl.multiple_of(k * 256 + core * 128, 128), 128)] = ret[
                k, :, pl.ds(pl.multiple_of(core * 128, 128), 128)
            ].T

        def step(k, carry):
            multiply(k)

            @pl.when(k >= 1)
            def _():
                sum_x(k - 1)

            @pl.when(k >= 2)
            def _():
                sum_y(k - 2)

            return carry

        lax.fori_loop(0, NB, step, 0)
        sum_x(NB - 1)
        sum_y(NB - 2)
        sum_y(NB - 1)

        def finish(k, carry):
            for j in range(1, 4):
                copy_a(k, j).wait_send()
            copy_b(k).wait_send()
            return_copy(k).wait_send()
            copy_t(k).wait_send()
            copy(
                tile.at[k], out.at[:, pl.ds(pl.multiple_of(k * 256 + 128 - core * 128, 128), 128)],
                ts.at[k], tr.at[k], sibling, col,
            ).wait_recv()
            return carry

        lax.fori_loop(0, NB, finish, 0)


def shards(design, species, species_weight):
    onehot = (
        species[:, None] == jnp.arange(species_weight.shape[0], dtype=jnp.int32)[None, :]
    ).astype(jnp.float32)
    row_weight = jnp.sum(onehot * species_weight[None, :], axis=1)
    weight = jnp.broadcast_to(row_weight[:, None], (DEPTH, 128))
    dma = pltpu.SemaphoreType.DMA
    vmem = pltpu.VMEM
    return pl.pallas_call(
        kernel,
        out_shape=jax.ShapeDtypeStruct((128, WIDTH), F32),
        in_specs=[pl.BlockSpec(memory_space=pl.ANY)] * 2,
        out_specs=pl.BlockSpec(memory_space=pltpu.VMEM),
        scratch_shapes=[
            vmem((2, DEPTH, WIDTH), BF),
            vmem((2, DEPTH, 128), F32),
            vmem((2 * DEPTH, WIDTH), BF),
            vmem((2 * DEPTH, WIDTH), BF),
            vmem((NB, 2 * DEPTH, 128), BF),
            vmem((128, 2 * DEPTH), BF),
            vmem((NB, 3, 128, 512), BF),
            vmem((NB, 3, 128, 512), BF),
            vmem((NB, 128, 512), F32),
            vmem((NB, 128, 256), F32),
            vmem((NB, 128, 256), F32),
            vmem((NB, 128, 256), F32),
            vmem((NB, 128, 256), F32),
            vmem((NB, 128, 128), F32),
            dma((2,)),
            dma, dma, dma, dma,
            dma((NB, 2)), dma((NB, 2)),
            dma((NB, 3)), dma((NB, 3)),
            dma((NB,)), dma((NB,)),
            dma((NB,)), dma((NB,)),
            dma((NB,)), dma((8,)),
        ],
        compiler_params=pltpu.CompilerParams(
            collective_id=0, has_side_effects=True, vmem_limit_bytes=56 * 2**20
        ),
        cost_estimate=pl.CostEstimate(flops=4 * 1536 * 2048 * 1024, bytes_accessed=8 * 2**20, transcendentals=0),
    )(design, weight)


def solution(mesh):
    placed = (P("row", "col"), P("row"), P())
    return jax.shard_map(
        shards, mesh=mesh, in_specs=placed, out_specs=P(("col", "row"), None), check_vma=False
    )
```

```python
import jax
import jax.numpy as jnp
from jax import lax
from jax.experimental import pallas as pl
from jax.experimental.pallas import tpu as pltpu
from jax.sharding import PartitionSpec as P

MESH = pl.DeviceIdType.MESH
BF = jnp.bfloat16
F32 = jnp.float32
DEPTH = 768
WIDTH = 2048
NB = 8
NORM = float(12288) ** -0.5


def kernel(
    design, weight, out,
    raw, wv, hi, lo, rbuf, rt, send_a, recv_a, own, send_b, recv_b, half, ret, tile, stage, recv_q,
    local_sem, ls, lr, ws, wr, rs, rr, as_, ar, bs, br, ts, tr, os_, orr, gs, gr,
):
    row = lax.axis_index("row")
    col = lax.axis_index("col")
    mirror = 15 - col
    beside = lax.rem(col + 8, 16)
    core = lax.rem(row, 2)
    chip = lax.div(row, 2)
    y = lax.rem(chip, 2)
    x = lax.div(chip, 2)
    sibling = row + 1 - 2 * core
    across = row + 2 - 4 * y
    computes = lax.rem(col, 2) == 1
    barrier = pltpu.get_barrier_semaphore()

    def copy(src, dst, ss, rs_, to_row, to_col):
        return pltpu.make_async_remote_copy(
            src_ref=src, dst_ref=dst, send_sem=ss, recv_sem=rs_, device_id=(to_row, to_col), device_id_type=MESH
        )

    def greet(to_row, to_col):
        pl.semaphore_signal(barrier, inc=1, device_id=(to_row, to_col), device_id_type=MESH)

    def row_at(j):
        return lax.rem(x + j, 4) * 4 + y * 2 + core

    def design_copy(k, c):
        return copy(
            design.at[:, pl.ds(pl.multiple_of(k * 256 + c * 128, 128), 128)],
            rbuf.at[k, pl.ds(pl.multiple_of(core * DEPTH, DEPTH), DEPTH), :],
            rs.at[k, c], rr.at[k, core], chip * 2 + c, mirror,
        )

    def stage_copy(i, c):
        return copy(
            design.at[:, pl.ds(pl.multiple_of((2 * i + 1) * 256 + c * 128, 128), 128)],
            stage.at[i, c], gs.at[i, c], gr.at[i, c], row, beside,
        )

    def forward_copy(i, c):
        return copy(
            stage.at[i, c], rbuf.at[2 * i + 1, pl.ds(pl.multiple_of(core * DEPTH, DEPTH), DEPTH), :],
            rs.at[2 * i + 1, c], rr.at[2 * i + 1, core], chip * 2 + c, 15 - beside,
        )

    def return_copy(k):
        return copy(ret.at[k], recv_q.at[chip], os_.at[k], orr.at[chip], 2 * k + core, mirror)

    @pl.when(jnp.logical_not(computes))
    def _():
        for q in range(8):
            greet(2 * q + core, mirror)
        greet(row, beside)
        pl.semaphore_wait(barrier, 5)
        for c in range(2):
            stage_copy(0, c).start()
        for c in range(2):
            design_copy(0, c).start()

        def step(i, carry):
            @pl.when(i < NB // 2 - 1)
            def _():
                for c in range(2):
                    stage_copy(i + 1, c).start()

            for c in range(2):
                stage_copy(i, c).wait_recv()
                forward_copy(i, c).start()

            @pl.when(i < NB // 2 - 1)
            def _():
                for c in range(2):
                    design_copy(2 * i + 2, c).start()

            for c in range(2):
                stage_copy(i, c).wait_send()
                design_copy(2 * i, c).wait_send()

            @pl.when(i >= 1)
            def _():
                for c in range(2):
                    forward_copy(i - 1, c).wait_send()

            return carry

        lax.fori_loop(0, NB // 2, step, 0)
        for c in range(2):
            forward_copy(NB // 2 - 1, c).wait_send()
        for q in range(8):
            copy(ret.at[0], recv_q.at[q], os_.at[0], orr.at[q], row, mirror).wait_recv()
            size = jnp.exp2(recv_q[q, 128:144, :].astype(F32)[0:1, :] - 15.0)
            out[:, q * 256 : q * 256 + 256] = recv_q[q, 0:128, :].astype(F32) * size

    @pl.when(computes)
    def _():
        greet(chip * 2, mirror)
        greet(chip * 2 + 1, mirror)
        for c in range(2):
            greet(chip * 2 + c, lax.rem(mirror + 8, 16))
        greet(sibling, col)
        greet(across, col)
        for j in range(1, 4):
            greet(row_at(j), col)
        mine = pltpu.make_async_copy(design, raw.at[core], local_sem.at[0])
        mine_w = pltpu.make_async_copy(weight, wv.at[core], local_sem.at[1])
        mine.start()
        mine_w.start()
        pl.semaphore_wait(barrier, 13)
        theirs = copy(design, raw.at[core], ls, lr, sibling, col)
        theirs_w = copy(weight, wv.at[core], ws, wr, sibling, col)
        theirs_w.start()
        theirs.start()

        def scale(s):
            def piece(i, carry):
                at = pl.ds(pl.multiple_of(i * 32, 32), 32)
                to = pl.ds(pl.multiple_of(s * DEPTH + i * 32, 32), 32)
                value = raw[s, at, :].astype(F32) * wv[s, at, 0:1]
                high = value.astype(BF)
                hi[to, :] = high
                lo[to, :] = (value - high.astype(F32)).astype(BF)
                return carry

            lax.fori_loop(0, DEPTH // 32, piece, 0)

        mine.wait()
        mine_w.wait()
        scale(core)
        theirs_w.wait()
        theirs.wait()
        scale(1 - core)

        def copy_a(k, j):
            return copy(send_a.at[k, j - 1], recv_a.at[k, j - 1], as_.at[k, j - 1], ar.at[k, j - 1], row_at(j), col)

        def copy_b(k):
            return copy(send_b.at[k], recv_b.at[k], bs.at[k], br.at[k], across, col)

        def copy_t(k):
            return copy(
                tile.at[k], out.at[:, pl.ds(pl.multiple_of(k * 256 + core * 128, 128), 128)], ts.at[k], tr.at[k], sibling, col
            )

        def multiply(k):
            for c in range(2):
                copy(
                    design.at[:, pl.ds(0, 128)], rbuf.at[k, pl.ds(c * DEPTH, DEPTH), :], rs.at[k, c], rr.at[k, c], row, mirror
                ).wait_recv()
            rt[...] = rbuf[k].T
            for j in (2, 1, 3, 0):
                at = pl.ds(pl.multiple_of(lax.rem(x + j, 4) * 512, 512), 512)
                part = jnp.dot(rt[...], hi[:, at], preferred_element_type=F32)
                part += jnp.dot(rt[...], lo[:, at], preferred_element_type=F32)
                if j:
                    send_a[k, j - 1] = part.astype(BF)
                    copy_a(k, j).start()
                else:
                    own[k] = part

        def sum_x(k):
            for j in range(1, 4):
                copy_a(k, j).wait_recv()
            at_mine = pl.ds(pl.multiple_of(y * 256, 256), 256)
            at_other = pl.ds(pl.multiple_of(256 - y * 256, 256), 256)

            def total(at):
                t = own[k, :, at]
                for j in range(3):
                    t += recv_a[k, j, :, at].astype(F32)
                return t

            send_b[k] = total(at_other)
            copy_b(k).start()
            half[k] = total(at_mine)

        def sum_y(k):
            copy_b(k).wait_recv()
            done = (half[k] + recv_b[k]) * NORM
            half[k] = done
            largest = jnp.max(jnp.max(jnp.abs(done), axis=0, keepdims=True), axis=1, keepdims=True)
            power = jnp.maximum(jnp.ceil(jnp.log2(jnp.maximum(largest, 1e-30))), -99.0)
            steps = jnp.clip(jnp.round(done * jnp.exp2(15.0 - power)), -32767.0, 32767.0)
            ret[k, 0:128, :] = steps.astype(jnp.int32).astype(jnp.int16)
            ret[k, 128:144, :] = jnp.broadcast_to(power, (16, 256)).astype(jnp.int32).astype(jnp.int16)
            return_copy(k).start()
            tile[k] = half[k, :, pl.ds(pl.multiple_of(128 - core * 128, 128), 128)].T
            copy_t(k).start()
            out[:, pl.ds(pl.multiple_of(k * 256 + core * 128, 128), 128)] = half[
                k, :, pl.ds(pl.multiple_of(core * 128, 128), 128)
            ].T

        def step(k, carry):
            multiply(k)

            @pl.when(k >= 1)
            def _():
                sum_x(k - 1)

            @pl.when(k >= 2)
            def _():
                sum_y(k - 2)

            return carry

        lax.fori_loop(0, NB, step, 0)
        sum_x(NB - 1)
        sum_y(NB - 2)
        sum_y(NB - 1)

        def finish(k, carry):
            for j in range(1, 4):
                copy_a(k, j).wait_send()
            copy_b(k).wait_send()
            return_copy(k).wait_send()
            copy_t(k).wait_send()
            copy(
                tile.at[k], out.at[:, pl.ds(pl.multiple_of(k * 256 + 128 - core * 128, 128), 128)],
                ts.at[k], tr.at[k], sibling, col,
            ).wait_recv()
            return carry

        lax.fori_loop(0, NB, finish, 0)


def shards(design, species, species_weight):
    onehot = (
        species[:, None] == jnp.arange(species_weight.shape[0], dtype=jnp.int32)[None, :]
    ).astype(jnp.float32)
    row_weight = jnp.sum(onehot * species_weight[None, :], axis=1)
    weight = jnp.broadcast_to(row_weight[:, None], (DEPTH, 128))
    dma = pltpu.SemaphoreType.DMA
    vmem = pltpu.VMEM
    return pl.pallas_call(
        kernel,
        out_shape=jax.ShapeDtypeStruct((128, WIDTH), F32),
        in_specs=[pl.BlockSpec(memory_space=pl.ANY)] * 2,
        out_specs=pl.BlockSpec(memory_space=pltpu.VMEM),
        scratch_shapes=[
            vmem((2, DEPTH, WIDTH), BF),
            vmem((2, DEPTH, 128), F32),
            vmem((2 * DEPTH, WIDTH), BF),
            vmem((2 * DEPTH, WIDTH), BF),
            vmem((NB, 2 * DEPTH, 128), BF),
            vmem((128, 2 * DEPTH), BF),
            vmem((NB, 3, 128, 512), BF),
            vmem((NB, 3, 128, 512), BF),
            vmem((NB, 128, 512), F32),
            vmem((NB, 128, 256), F32),
            vmem((NB, 128, 256), F32),
            vmem((NB, 128, 256), F32),
            vmem((NB, 144, 256), jnp.int16),
            vmem((NB, 128, 128), F32),
            vmem((NB // 2, 2, DEPTH, 128), BF),
            vmem((8, 144, 256), jnp.int16),
            dma((2,)),
            dma, dma, dma, dma,
            dma((NB, 2)), dma((NB, 2)),
            dma((NB, 3)), dma((NB, 3)),
            dma((NB,)), dma((NB,)),
            dma((NB,)), dma((NB,)),
            dma((NB,)), dma((8,)),
            dma((NB // 2, 2)), dma((NB // 2, 2)),
        ],
        compiler_params=pltpu.CompilerParams(
            collective_id=0, has_side_effects=True, vmem_limit_bytes=56 * 2**20
        ),
        cost_estimate=pl.CostEstimate(flops=4 * 1536 * 2048 * 1024, bytes_accessed=8 * 2**20, transcendentals=0),
    )(design, weight)


def solution(mesh):
    placed = (P("row", "col"), P("row"), P())
    return jax.shard_map(
        shards, mesh=mesh, in_specs=placed, out_specs=P(("col", "row"), None), check_vma=False
    )
```

```python
import jax
import jax.numpy as jnp
from jax import lax
from jax.experimental import pallas as pl
from jax.experimental.pallas import tpu as pltpu
from jax.sharding import PartitionSpec as P

MESH = pl.DeviceIdType.MESH
BF = jnp.bfloat16
F32 = jnp.float32
DEPTH = 768
WIDTH = 2048
NB = 8
NORM = float(12288) ** -0.5


def kernel(
    design, species, species_weight, out,
    raw, wv, hi, lo, rbuf, rt, send_a, recv_a, own, send_b, recv_b, half, ret, tile, stage, recv_q, species_here, weight_here,
    local_sem, ls, lr, ws, wr, rs, rr, as_, ar, bs, br, ts, tr, os_, orr, gs, gr,
):
    row = lax.axis_index("row")
    col = lax.axis_index("col")
    mirror = 15 - col
    beside = lax.rem(col + 8, 16)
    core = lax.rem(row, 2)
    chip = lax.div(row, 2)
    y = lax.rem(chip, 2)
    x = lax.div(chip, 2)
    sibling = row + 1 - 2 * core
    across = row + 2 - 4 * y
    computes = lax.rem(col, 2) == 1
    barrier = pltpu.get_barrier_semaphore()

    def copy(src, dst, ss, rs_, to_row, to_col):
        return pltpu.make_async_remote_copy(
            src_ref=src, dst_ref=dst, send_sem=ss, recv_sem=rs_, device_id=(to_row, to_col), device_id_type=MESH
        )

    def greet(to_row, to_col):
        pl.semaphore_signal(barrier, inc=1, device_id=(to_row, to_col), device_id_type=MESH)

    def row_at(j):
        return lax.rem(x + j, 4) * 4 + y * 2 + core

    def design_copy(k, c):
        return copy(
            design.at[:, pl.ds(pl.multiple_of(k * 256 + c * 128, 128), 128)],
            rbuf.at[k, pl.ds(pl.multiple_of(core * DEPTH, DEPTH), DEPTH), :],
            rs.at[k, c], rr.at[k, core], chip * 2 + c, mirror,
        )

    def stage_copy(i, c):
        return copy(
            design.at[:, pl.ds(pl.multiple_of((2 * i + 1) * 256 + c * 128, 128), 128)],
            stage.at[i, c], gs.at[i, c], gr.at[i, c], row, beside,
        )

    def forward_copy(i, c):
        return copy(
            stage.at[i, c], rbuf.at[2 * i + 1, pl.ds(pl.multiple_of(core * DEPTH, DEPTH), DEPTH), :],
            rs.at[2 * i + 1, c], rr.at[2 * i + 1, core], chip * 2 + c, 15 - beside,
        )

    def return_copy(k):
        return copy(ret.at[k], recv_q.at[chip], os_.at[k], orr.at[chip], 2 * k + core, mirror)

    @pl.when(jnp.logical_not(computes))
    def _():
        for q in range(8):
            greet(2 * q + core, mirror)
        greet(row, beside)
        pl.semaphore_wait(barrier, 5)
        for c in range(2):
            stage_copy(0, c).start()
        for c in range(2):
            design_copy(0, c).start()

        def step(i, carry):
            @pl.when(i < NB // 2 - 1)
            def _():
                for c in range(2):
                    stage_copy(i + 1, c).start()

            for c in range(2):
                stage_copy(i, c).wait_recv()
                forward_copy(i, c).start()

            @pl.when(i < NB // 2 - 1)
            def _():
                for c in range(2):
                    design_copy(2 * i + 2, c).start()

            for c in range(2):
                stage_copy(i, c).wait_send()
                design_copy(2 * i, c).wait_send()

            @pl.when(i >= 1)
            def _():
                for c in range(2):
                    forward_copy(i - 1, c).wait_send()

            return carry

        lax.fori_loop(0, NB // 2, step, 0)
        for c in range(2):
            forward_copy(NB // 2 - 1, c).wait_send()
        for q in range(8):
            copy(ret.at[0], recv_q.at[q], os_.at[0], orr.at[q], row, mirror).wait_recv()
            size = jnp.exp2(recv_q[q, 128:144, :].astype(F32)[0:1, :] - 15.0)
            out[:, q * 256 : q * 256 + 256] = recv_q[q, 0:128, :].astype(F32) * size

    @pl.when(computes)
    def _():
        greet(chip * 2, mirror)
        greet(chip * 2 + 1, mirror)
        for c in range(2):
            greet(chip * 2 + c, lax.rem(mirror + 8, 16))
        greet(sibling, col)
        greet(across, col)
        for j in range(1, 4):
            greet(row_at(j), col)
        mine = pltpu.make_async_copy(design, raw.at[core], local_sem.at[0])
        mine.start()
        kinds = pltpu.make_async_copy(species, species_here, local_sem.at[1])
        kinds.start()
        by_kind = pltpu.make_async_copy(species_weight, weight_here, local_sem.at[2])
        by_kind.start()
        kinds.wait()
        by_kind.wait()
        for i in range(DEPTH // 128):
            kind = species_here[i * 128 : i * 128 + 128].reshape(1, 128)
            value = jnp.zeros((1, 128), F32)
            for n in range(10):
                value = jnp.where(kind == n, weight_here[n], value)
            wv[core, i * 128 : i * 128 + 128, :] = jnp.broadcast_to(value, (128, 128)).T
        pl.semaphore_wait(barrier, 13)
        theirs = copy(design, raw.at[core], ls, lr, sibling, col)
        theirs_w = copy(wv.at[core], wv.at[core], ws, wr, sibling, col)
        theirs_w.start()
        theirs.start()

        def scale(s):
            def piece(i, carry):
                at = pl.ds(pl.multiple_of(i * 32, 32), 32)
                to = pl.ds(pl.multiple_of(s * DEPTH + i * 32, 32), 32)
                value = raw[s, at, :].astype(F32) * wv[s, at, 0:1]
                high = value.astype(BF)
                hi[to, :] = high
                lo[to, :] = (value - high.astype(F32)).astype(BF)
                return carry

            lax.fori_loop(0, DEPTH // 32, piece, 0)

        mine.wait()
        scale(core)
        theirs_w.wait()
        theirs.wait()
        scale(1 - core)

        def copy_a(k, j):
            return copy(send_a.at[k, j - 1], recv_a.at[k, j - 1], as_.at[k, j - 1], ar.at[k, j - 1], row_at(j), col)

        def copy_b(k):
            return copy(send_b.at[k], recv_b.at[k], bs.at[k], br.at[k], across, col)

        def copy_t(k):
            return copy(
                tile.at[k], out.at[:, pl.ds(pl.multiple_of(k * 256 + core * 128, 128), 128)], ts.at[k], tr.at[k], sibling, col
            )

        def multiply(k):
            for c in range(2):
                copy(
                    design.at[:, pl.ds(0, 128)], rbuf.at[k, pl.ds(c * DEPTH, DEPTH), :], rs.at[k, c], rr.at[k, c], row, mirror
                ).wait_recv()
            rt[...] = rbuf[k].T
            for j in (2, 1, 3, 0):
                at = pl.ds(pl.multiple_of(lax.rem(x + j, 4) * 512, 512), 512)
                part = jnp.dot(rt[...], hi[:, at], preferred_element_type=F32)
                part += jnp.dot(rt[...], lo[:, at], preferred_element_type=F32)
                if j:
                    send_a[k, j - 1] = part.astype(BF)
                    copy_a(k, j).start()
                else:
                    own[k] = part

        def sum_x(k):
            for j in range(1, 4):
                copy_a(k, j).wait_recv()
            at_mine = pl.ds(pl.multiple_of(y * 256, 256), 256)
            at_other = pl.ds(pl.multiple_of(256 - y * 256, 256), 256)

            def total(at):
                t = own[k, :, at]
                for j in range(3):
                    t += recv_a[k, j, :, at].astype(F32)
                return t

            send_b[k] = total(at_other)
            copy_b(k).start()
            half[k] = total(at_mine)

        def sum_y(k, now=False):
            copy_b(k).wait_recv()
            done = (half[k] + recv_b[k]) * NORM
            half[k] = done
            largest = jnp.max(jnp.max(jnp.abs(done), axis=0, keepdims=True), axis=1, keepdims=True)
            power = jnp.maximum(jnp.ceil(jnp.log2(jnp.maximum(largest, 1e-30))), -99.0)
            steps = jnp.clip(jnp.round(done * jnp.exp2(15.0 - power)), -32767.0, 32767.0)
            ret[k, 0:128, :] = steps.astype(jnp.int32).astype(jnp.int16)
            ret[k, 128:144, :] = jnp.broadcast_to(power, (16, 256)).astype(jnp.int32).astype(jnp.int16)
            if now:
                return_copy(k).start()
            tile[k] = half[k, :, pl.ds(pl.multiple_of(128 - core * 128, 128), 128)].T
            copy_t(k).start()
            out[:, pl.ds(pl.multiple_of(k * 256 + core * 128, 128), 128)] = half[
                k, :, pl.ds(pl.multiple_of(core * 128, 128), 128)
            ].T

        def step(k, carry):
            multiply(k)

            @pl.when(k >= 1)
            def _():
                sum_x(k - 1)

            @pl.when(k >= 2)
            def _():
                sum_y(k - 2)

            return carry

        lax.fori_loop(0, NB, step, 0)
        for i in range(NB - 2):
            return_copy(lax.rem(chip + i, NB - 2)).start()
        sum_x(NB - 1)
        sum_y(NB - 2, True)
        sum_y(NB - 1, True)

        def finish(k, carry):
            for j in range(1, 4):
                copy_a(k, j).wait_send()
            copy_b(k).wait_send()
            return_copy(k).wait_send()
            copy_t(k).wait_send()
            copy(
                tile.at[k], out.at[:, pl.ds(pl.multiple_of(k * 256 + 128 - core * 128, 128), 128)],
                ts.at[k], tr.at[k], sibling, col,
            ).wait_recv()
            return carry

        lax.fori_loop(0, NB, finish, 0)


def shards(design, species, species_weight):
    dma = pltpu.SemaphoreType.DMA
    vmem = pltpu.VMEM
    return pl.pallas_call(
        kernel,
        out_shape=jax.ShapeDtypeStruct((128, WIDTH), F32),
        in_specs=[pl.BlockSpec(memory_space=pltpu.HBM)] * 3,
        out_specs=pl.BlockSpec(memory_space=pltpu.VMEM),
        scratch_shapes=[
            vmem((2, DEPTH, WIDTH), BF),
            vmem((2, DEPTH, 128), F32),
            vmem((2 * DEPTH, WIDTH), BF),
            vmem((2 * DEPTH, WIDTH), BF),
            vmem((NB, 2 * DEPTH, 128), BF),
            vmem((128, 2 * DEPTH), BF),
            vmem((NB, 3, 128, 512), BF),
            vmem((NB, 3, 128, 512), BF),
            vmem((NB, 128, 512), F32),
            vmem((NB, 128, 256), F32),
            vmem((NB, 128, 256), F32),
            vmem((NB, 128, 256), F32),
            vmem((NB, 144, 256), jnp.int16),
            vmem((NB, 128, 128), F32),
            vmem((NB // 2, 2, DEPTH, 128), BF),
            vmem((8, 144, 256), jnp.int16),
            vmem((DEPTH,), jnp.int32),
            pltpu.SMEM((10,), F32),
            dma((3,)),
            dma, dma, dma, dma,
            dma((NB, 2)), dma((NB, 2)),
            dma((NB, 3)), dma((NB, 3)),
            dma((NB,)), dma((NB,)),
            dma((NB,)), dma((NB,)),
            dma((NB,)), dma((8,)),
            dma((NB // 2, 2)), dma((NB // 2, 2)),
        ],
        compiler_params=pltpu.CompilerParams(
            collective_id=0, has_side_effects=True, vmem_limit_bytes=50 * 2**20
        ),
        cost_estimate=pl.CostEstimate(flops=4 * 1536 * 2048 * 1024, bytes_accessed=8 * 2**20, transcendentals=0),
    )(*(pltpu.with_memory_space_constraint(a, pltpu.HBM) for a in (design, species, species_weight)))


def solution(mesh):
    placed = (P("row", "col"), P("row"), P())
    return jax.shard_map(
        shards, mesh=mesh, in_specs=placed, out_specs=P(("col", "row"), None), check_vma=False
    )
```

```python
import jax
import jax.numpy as jnp
from jax import lax
from jax.experimental import pallas as pl
from jax.experimental.pallas import tpu as pltpu
from jax.sharding import PartitionSpec as P

MESH = pl.DeviceIdType.MESH
BF = jnp.bfloat16
F32 = jnp.float32
DEPTH = 768
WIDTH = 2048
NB = 8
LAST = NB - 1
NORM = float(12288) ** -0.5


def kernel(
    design, species, species_weight, out,
    raw, wv, hi, lo, rbuf, rt, send_a, recv_a, own, send_b, recv_b, half, ret, tile, stage, recv_q, species_here, weight_here,
    mix, gathered, ret_last, send_d, recv_d,
    local_sem, ls, lr, ws, wr, rs, rr, as_, ar, bs, br, ts, tr, os_, orr, gs, gr, ds_, dr, fs, fr,
):
    row = lax.axis_index("row")
    col = lax.axis_index("col")
    mirror = 15 - col
    beside = lax.rem(col + 8, 16)
    core = lax.rem(row, 2)
    chip = lax.div(row, 2)
    y = lax.rem(chip, 2)
    x = lax.div(chip, 2)
    sibling = row + 1 - 2 * core
    across = row + 2 - 4 * y
    computes = lax.rem(col, 2) == 1
    barrier = pltpu.get_barrier_semaphore()

    def copy(src, dst, ss, rs_, to_row, to_col):
        return pltpu.make_async_remote_copy(
            src_ref=src, dst_ref=dst, send_sem=ss, recv_sem=rs_, device_id=(to_row, to_col), device_id_type=MESH
        )

    def greet(to_row, to_col):
        pl.semaphore_signal(barrier, inc=1, device_id=(to_row, to_col), device_id_type=MESH)

    def chip_at(j, d):
        return lax.rem(x + j, 4) * 2 + lax.rem(y + d, 2)

    mine_128 = pl.ds(pl.multiple_of(core * 128, 128), 128)
    other_128 = pl.ds(pl.multiple_of(128 - core * 128, 128), 128)
    my_rows = pl.ds(pl.multiple_of(core * DEPTH, DEPTH), DEPTH)

    def design_copy(k, c):
        return copy(mix.at[k, c], rbuf.at[k, my_rows, :], rs.at[k, c], rr.at[k, core], chip * 2 + c, mirror)

    def stage_copy(i, c):
        return copy(mix.at[2 * i + 1, c], stage.at[i, c], gs.at[i, c], gr.at[i, c], row, beside)

    def forward_copy(i, c):
        k = 2 * i + 1
        return copy(stage.at[i, c], rbuf.at[k, my_rows, :], rs.at[k, c], rr.at[k, core], chip * 2 + c, 15 - beside)

    def return_copy(q):
        return copy(ret.at[q], recv_q.at[chip, pl.ds(0, 112), :], os_.at[q], orr.at[chip], 2 * q + core, mirror)

    def return_last(q):
        return copy(ret_last.at[q], recv_q.at[chip, pl.ds(112, 48), :], fs.at[q], fr.at[chip], 2 * q + core, mirror)

    @pl.when(jnp.logical_not(computes))
    def _():
        for q in range(8):
            greet(2 * q + core, mirror)
        greet(row, beside)
        here = pltpu.make_async_copy(design, raw.at[0], local_sem.at[0])
        here.start()

        def mixing(k, carry):
            a = lax.broadcasted_iota(jnp.int32, (1024, 128), 0)
            b = lax.broadcasted_iota(jnp.int32, (1024, 128), 1)
            wanted = lax.div(b, 16) * 128 + k * 16 + lax.rem(b, 16)
            order = jnp.where(a == wanted, 1.0, 0.0).astype(BF)
            for c in range(2):
                found = jnp.concatenate([raw[0, :, q * 256 + c * 128 : q * 256 + c * 128 + 128] for q in range(8)], axis=1)
                mix[k, c] = jnp.dot(found, order, preferred_element_type=F32).astype(BF)
            return carry

        here.wait()
        lax.fori_loop(0, 2, mixing, 0)
        pl.semaphore_wait(barrier, 5)
        for c in range(2):
            stage_copy(0, c).start()
        for c in range(2):
            design_copy(0, c).start()
        lax.fori_loop(2, 4, mixing, 0)
        for c in range(2):
            stage_copy(1, c).start()
        lax.fori_loop(4, NB, mixing, 0)

        for i in range(NB // 2):
            if 1 <= i < NB // 2 - 1:
                for c in range(2):
                    stage_copy(i + 1, c).start()
            for c in range(2):
                stage_copy(i, c).wait_recv()
                forward_copy(i, c).start()
            if i < NB // 2 - 1:
                for c in range(2):
                    design_copy(2 * i + 2, c).start()
            for c in range(2):
                stage_copy(i, c).wait_send()
                design_copy(2 * i, c).wait_send()
                if i >= 1:
                    forward_copy(i - 1, c).wait_send()
        for c in range(2):
            forward_copy(NB // 2 - 1, c).wait_send()

        def unpack(q, rows, first, to):
            size = jnp.exp2(recv_q[q, first + rows : first + rows + 16, :].astype(F32)[0:1, :] - 15.0)
            out[to : to + rows, q * 256 : q * 256 + 256] = recv_q[q, first : first + rows, :].astype(F32) * size

        for q in range(8):
            copy(ret.at[0], recv_q.at[q, pl.ds(0, 112), :], os_.at[0], orr.at[q], row, mirror).wait_recv()
            unpack(q, 96, 0, 0)
        for q in range(8):
            copy(ret_last.at[0], recv_q.at[q, pl.ds(112, 48), :], fs.at[0], fr.at[q], row, mirror).wait_recv()
            unpack(q, 32, 112, 96)

    @pl.when(computes)
    def _():
        for c in range(2):
            greet(chip * 2 + c, mirror)
        for c in range(2):
            greet(chip * 2 + c, lax.rem(mirror + 8, 16))
        greet(sibling, col)
        for n in range(1, 8):
            greet(chip_at(n // 2, n % 2) * 2 + core, col)
        mine = pltpu.make_async_copy(design, raw.at[core], local_sem.at[0])
        mine.start()
        kinds = pltpu.make_async_copy(species, species_here, local_sem.at[1])
        kinds.start()
        by_kind = pltpu.make_async_copy(species_weight, weight_here, local_sem.at[2])
        by_kind.start()
        kinds.wait()
        by_kind.wait()
        for i in range(DEPTH // 128):
            kind = species_here[i * 128 : i * 128 + 128].reshape(1, 128)
            value = jnp.zeros((1, 128), F32)
            for n in range(10):
                value = jnp.where(kind == n, weight_here[n], value)
            wv[core, i * 128 : i * 128 + 128, :] = jnp.broadcast_to(value, (128, 128)).T
        pl.semaphore_wait(barrier, 16)
        theirs = copy(design, raw.at[core], ls, lr, sibling, col)
        theirs_w = copy(wv.at[core], wv.at[core], ws, wr, sibling, col)
        theirs_w.start()
        theirs.start()

        def scale(s):
            def some(i, carry):
                at = pl.ds(pl.multiple_of(i * 32, 32), 32)
                to = pl.ds(pl.multiple_of(s * DEPTH + i * 32, 32), 32)
                value = raw[s, at, :].astype(F32) * wv[s, at, 0:1]
                high = value.astype(BF)
                hi[to, :] = high
                lo[to, :] = (value - high.astype(F32)).astype(BF)
                return carry

            lax.fori_loop(0, DEPTH // 32, some, 0)

        mine.wait()
        scale(core)
        theirs_w.wait()
        theirs.wait()
        scale(1 - core)

        def copy_a(k, j):
            return copy(
                send_a.at[k, j - 1], recv_a.at[k, j - 1], as_.at[k, j - 1], ar.at[k, j - 1], chip_at(j, 0) * 2 + core, col
            )

        def copy_b(k):
            return copy(send_b.at[k], recv_b.at[k], bs.at[k], br.at[k], across, col)

        def copy_d(n):
            return copy(
                send_d.at[n - 1], recv_d.at[n - 1], ds_.at[n - 1], dr.at[n - 1], chip_at(n // 2, n % 2) * 2 + core, col
            )

        def copy_t(q, c):
            return copy(
                tile.at[q], out.at[:, pl.ds(pl.multiple_of(q * 256 + c * 128, 128), 128)], ts.at[q], tr.at[q], sibling, col
            )

        def arrived(k):
            for c in range(2):
                copy(
                    mix.at[k, c], rbuf.at[k, pl.ds(c * DEPTH, DEPTH), :], rs.at[k, c], rr.at[k, c], row, mirror
                ).wait_recv()
            rt[...] = rbuf[k].T

        def product(at):
            part = jnp.dot(rt[...], hi[:, at], preferred_element_type=F32)
            return part + jnp.dot(rt[...], lo[:, at], preferred_element_type=F32)

        def multiply(k):
            arrived(k)
            for j in (2, 1, 3, 0):
                part = product(pl.ds(pl.multiple_of(lax.rem(x + j, 4) * 512, 512), 512))
                if j:
                    send_a[k, j - 1] = part.astype(BF)
                    copy_a(k, j).start()
                else:
                    own[k] = part

        def sum_x(k):
            for j in range(1, 4):
                copy_a(k, j).wait_recv()
            at_mine = pl.ds(pl.multiple_of(y * 256, 256), 256)
            at_other = pl.ds(pl.multiple_of(256 - y * 256, 256), 256)

            def total(at):
                t = own[k, :, at]
                for j in range(3):
                    t += recv_a[k, j, :, at].astype(F32)
                return t

            send_b[k] = total(at_other)
            copy_b(k).start()
            half[k] = total(at_mine)

        def pack(done, to, rows):
            largest = jnp.max(jnp.max(jnp.abs(done), axis=0, keepdims=True), axis=1, keepdims=True)
            power = jnp.maximum(jnp.ceil(jnp.log2(jnp.maximum(largest, 1e-30))), -99.0)
            steps = jnp.clip(jnp.round(done * jnp.exp2(15.0 - power)), -32767.0, 32767.0)
            to[0:rows, :] = steps.astype(jnp.int32).astype(jnp.int16)
            to[rows : rows + 16, :] = jnp.broadcast_to(power, (16, 256)).astype(jnp.int32).astype(jnp.int16)

        def place(q, values):
            tile[q] = values[:, other_128].T
            copy_t(q, core).start()
            out[:, pl.ds(pl.multiple_of(q * 256 + core * 128, 128), 128)] = values[:, mine_128].T

        def spread(k, done):
            at = pl.ds(pl.multiple_of(k * 16, 16), 16)
            for q in range(8):
                gathered[q, at, :] = done[q * 16 : q * 16 + 16, :]

        def sum_y(k):
            copy_b(k).wait_recv()
            spread(k, (half[k] + recv_b[k]) * NORM)

        def step(k, carry):
            multiply(k)

            @pl.when(k >= 1)
            def _():
                sum_x(k - 1)

            @pl.when(k >= 2)
            def _():
                sum_y(k - 2)

            return carry

        lax.fori_loop(0, LAST, step, 0)
        sum_y(LAST - 2)
        for q in range(8):
            pack(gathered[q, 0:96, :], ret.at[q], 96)

        arrived(LAST)
        for n in range(8):
            return_copy(lax.rem(chip + n, 8)).start()
        for n in (5, 4, 3, 2, 7, 6, 1, 0):
            part = product(pl.ds(pl.multiple_of(chip_at(n // 2, n % 2) * 256, 256), 256))
            if n:
                send_d[n - 1] = part.astype(BF)
                copy_d(n).start()
            else:
                half[LAST] = part
        sum_x(LAST - 1)
        total = half[LAST]
        for n in range(1, 8):
            copy_d(n).wait_recv()
            total += recv_d[n - 1].astype(F32)
        sum_y(LAST - 1)
        spread(LAST, total * NORM)
        for n in range(8):
            q = lax.rem(chip + n, 8)
            pack(gathered[q, 96:128, :], ret_last.at[q], 32)
            return_last(q).start()
        for q in range(8):
            place(q, gathered.at[q])

        def finish(k, carry):
            for j in range(1, 4):
                copy_a(k, j).wait_send()
            copy_b(k).wait_send()
            return carry

        lax.fori_loop(0, LAST, finish, 0)
        for n in range(1, 8):
            copy_d(n).wait_send()
        for q in range(8):
            return_copy(q).wait_send()
            return_last(q).wait_send()
            copy_t(q, core).wait_send()
            copy_t(q, 1 - core).wait_recv()


def shards(design, species, species_weight):
    dma = pltpu.SemaphoreType.DMA
    vmem = pltpu.VMEM
    return pl.pallas_call(
        kernel,
        out_shape=jax.ShapeDtypeStruct((128, WIDTH), F32),
        in_specs=[pl.BlockSpec(memory_space=pltpu.HBM)] * 3,
        out_specs=pl.BlockSpec(memory_space=pltpu.VMEM),
        scratch_shapes=[
            vmem((2, DEPTH, WIDTH), BF),
            vmem((2, DEPTH, 128), F32),
            vmem((2 * DEPTH, WIDTH), BF),
            vmem((2 * DEPTH, WIDTH), BF),
            vmem((NB, 2 * DEPTH, 128), BF),
            vmem((128, 2 * DEPTH), BF),
            vmem((LAST, 3, 128, 512), BF),
            vmem((LAST, 3, 128, 512), BF),
            vmem((LAST, 128, 512), F32),
            vmem((LAST, 128, 256), F32),
            vmem((LAST, 128, 256), F32),
            vmem((NB, 128, 256), F32),
            vmem((8, 112, 256), jnp.int16),
            vmem((NB, 128, 128), F32),
            vmem((NB // 2, 2, DEPTH, 128), BF),
            vmem((8, 160, 256), jnp.int16),
            vmem((DEPTH,), jnp.int32),
            pltpu.SMEM((10,), F32),
            vmem((NB, 2, DEPTH, 128), BF),
            vmem((8, 128, 256), F32),
            vmem((8, 48, 256), jnp.int16),
            vmem((7, 128, 256), BF),
            vmem((7, 128, 256), BF),
            dma((3,)),
            dma, dma, dma, dma,
            dma((NB, 2)), dma((NB, 2)),
            dma((LAST, 3)), dma((LAST, 3)),
            dma((LAST,)), dma((LAST,)),
            dma((NB,)), dma((NB,)),
            dma((8,)), dma((8,)),
            dma((NB // 2, 2)), dma((NB // 2, 2)),
            dma((7,)), dma((7,)),
            dma((8,)), dma((8,)),
        ],
        compiler_params=pltpu.CompilerParams(
            collective_id=0, has_side_effects=True, vmem_limit_bytes=50 * 2**20
        ),
        cost_estimate=pl.CostEstimate(flops=4 * 1536 * 2048 * 1024, bytes_accessed=8 * 2**20, transcendentals=0),
    )(*(pltpu.with_memory_space_constraint(a, pltpu.HBM) for a in (design, species, species_weight)))


def solution(mesh):
    placed = (P("row", "col"), P("row"), P())
    return jax.shard_map(
        shards, mesh=mesh, in_specs=placed, out_specs=P(("col", "row"), None), check_vma=False
    )
```

```python
import jax
import jax.numpy as jnp
from jax import lax
from jax.experimental import pallas as pl
from jax.experimental.pallas import tpu as pltpu
from jax.sharding import PartitionSpec as P

MESH = pl.DeviceIdType.MESH
BF = jnp.bfloat16
F32 = jnp.float32
DEPTH = 768
WIDTH = 2048
NB = 8
LAST = NB - 1
NORM = float(12288) ** -0.5


def kernel(
    design, species, species_weight, out,
    raw, wv, hi, lo, rbuf, rt, send_a, recv_a, own, send_b, recv_b, half, ret, tile, stage, recv_q, species_here, weight_here,
    mix, gathered, ret_last, recv_l, send_d, recv_d,
    local_sem, ls, lr, ws, wr, rs, rr, as_, ar, bs, br, ts, tr, os_, orr, gs, gr, ds_, dr, fs, fr,
):
    row = lax.axis_index("row")
    col = lax.axis_index("col")
    mirror = 15 - col
    beside = lax.rem(col + 8, 16)
    core = lax.rem(row, 2)
    chip = lax.div(row, 2)
    y = lax.rem(chip, 2)
    x = lax.div(chip, 2)
    sibling = row + 1 - 2 * core
    across = row + 2 - 4 * y
    computes = lax.rem(col, 2) == 1
    barrier = pltpu.get_barrier_semaphore()

    def copy(src, dst, ss, rs_, to_row, to_col):
        return pltpu.make_async_remote_copy(
            src_ref=src, dst_ref=dst, send_sem=ss, recv_sem=rs_, device_id=(to_row, to_col), device_id_type=MESH
        )

    def greet(to_row, to_col):
        pl.semaphore_signal(barrier, inc=1, device_id=(to_row, to_col), device_id_type=MESH)

    def chip_at(j, d):
        return lax.rem(x + j, 4) * 2 + lax.rem(y + d, 2)

    mine_128 = pl.ds(pl.multiple_of(core * 128, 128), 128)
    other_128 = pl.ds(pl.multiple_of(128 - core * 128, 128), 128)
    my_rows = pl.ds(pl.multiple_of(core * DEPTH, DEPTH), DEPTH)

    def design_copy(k, c):
        return copy(mix.at[k, c], rbuf.at[k, my_rows, :], rs.at[k, c], rr.at[k, core], chip * 2 + c, mirror)

    def stage_copy(i, c):
        return copy(mix.at[2 * i + 1, c], stage.at[i, c], gs.at[i, c], gr.at[i, c], row, beside)

    def forward_copy(i, c):
        k = 2 * i + 1
        return copy(stage.at[i, c], rbuf.at[k, my_rows, :], rs.at[k, c], rr.at[k, core], chip * 2 + c, 15 - beside)

    def return_copy(q):
        return copy(ret.at[q], recv_q.at[chip], os_.at[q], orr.at[chip], 2 * q + core, mirror)

    def return_last(q):
        return copy(ret_last.at[q], recv_l.at[chip], fs.at[q], fr.at[chip], 2 * q + core, mirror)

    @pl.when(jnp.logical_not(computes))
    def _():
        for q in range(8):
            greet(2 * q + core, mirror)
        greet(row, beside)
        here = pltpu.make_async_copy(design, raw.at[0], local_sem.at[0])
        here.start()

        def mixing(k, carry):
            a = lax.broadcasted_iota(jnp.int32, (1024, 128), 0)
            b = lax.broadcasted_iota(jnp.int32, (1024, 128), 1)
            wanted = lax.div(b, 16) * 128 + k * 16 + lax.rem(b, 16)
            order = jnp.where(a == wanted, 1.0, 0.0).astype(BF)
            for c in range(2):
                found = jnp.concatenate([raw[0, :, q * 256 + c * 128 : q * 256 + c * 128 + 128] for q in range(8)], axis=1)
                mix[k, c] = jnp.dot(found, order, preferred_element_type=F32).astype(BF)
            return carry

        here.wait()
        lax.fori_loop(0, 2, mixing, 0)
        pl.semaphore_wait(barrier, 5)
        for c in range(2):
            stage_copy(0, c).start()
        for c in range(2):
            design_copy(0, c).start()
        lax.fori_loop(2, 4, mixing, 0)
        for c in range(2):
            stage_copy(1, c).start()
        lax.fori_loop(4, NB, mixing, 0)

        for i in range(NB // 2):
            if 1 <= i < NB // 2 - 1:
                for c in range(2):
                    stage_copy(i + 1, c).start()
            for c in range(2):
                stage_copy(i, c).wait_recv()
                forward_copy(i, c).start()
            if i < NB // 2 - 1:
                for c in range(2):
                    design_copy(2 * i + 2, c).start()
            for c in range(2):
                stage_copy(i, c).wait_send()
                design_copy(2 * i, c).wait_send()
                if i >= 1:
                    forward_copy(i - 1, c).wait_send()
        for c in range(2):
            forward_copy(NB // 2 - 1, c).wait_send()

        for q in range(8):
            copy(ret.at[0], recv_q.at[q], os_.at[0], orr.at[q], row, mirror).wait_recv()
            size = jnp.exp2(recv_q[q, 192:208, :].astype(F32)[0:1, :] - 15.0)
            for h in range(2):
                at = q * 256 + h * 128
                out[0:96, at : at + 128] = recv_q[q, h * 96 : h * 96 + 96, :].astype(F32) * size
        for q in range(8):
            copy(ret_last.at[0], recv_l.at[q], fs.at[0], fr.at[q], row, mirror).wait_recv()
            out[96:128, q * 256 : q * 256 + 256] = recv_l[q].astype(F32)

    @pl.when(computes)
    def _():
        for c in range(2):
            greet(chip * 2 + c, mirror)
        for c in range(2):
            greet(chip * 2 + c, lax.rem(mirror + 8, 16))
        greet(sibling, col)
        for n in range(1, 8):
            greet(chip_at(n // 2, n % 2) * 2 + core, col)
        mine = pltpu.make_async_copy(design, raw.at[core], local_sem.at[0])
        mine.start()
        kinds = pltpu.make_async_copy(species, species_here, local_sem.at[1])
        kinds.start()
        by_kind = pltpu.make_async_copy(species_weight, weight_here, local_sem.at[2])
        by_kind.start()
        kinds.wait()
        by_kind.wait()
        for i in range(DEPTH // 128):
            kind = species_here[i * 128 : i * 128 + 128].reshape(1, 128)
            value = jnp.zeros((1, 128), F32)
            for n in range(10):
                value = jnp.where(kind == n, weight_here[n], value)
            wv[core, i * 128 : i * 128 + 128, :] = jnp.broadcast_to(value, (128, 128)).T
        pl.semaphore_wait(barrier, 16)
        theirs = copy(design, raw.at[core], ls, lr, sibling, col)
        theirs_w = copy(wv.at[core], wv.at[core], ws, wr, sibling, col)
        theirs_w.start()
        theirs.start()

        def scale(s):
            def some(i, carry):
                at = pl.ds(pl.multiple_of(i * 32, 32), 32)
                to = pl.ds(pl.multiple_of(s * DEPTH + i * 32, 32), 32)
                value = raw[s, at, :].astype(F32) * wv[s, at, 0:1]
                high = value.astype(BF)
                hi[to, :] = high
                lo[to, :] = (value - high.astype(F32)).astype(BF)
                return carry

            lax.fori_loop(0, DEPTH // 32, some, 0)

        mine.wait()
        scale(core)
        theirs_w.wait()
        theirs.wait()
        scale(1 - core)

        def copy_a(k, j):
            return copy(
                send_a.at[k, j - 1], recv_a.at[k, j - 1], as_.at[k, j - 1], ar.at[k, j - 1], chip_at(j, 0) * 2 + core, col
            )

        def copy_b(k):
            return copy(send_b.at[k], recv_b.at[k], bs.at[k], br.at[k], across, col)

        def copy_d(n):
            return copy(
                send_d.at[n - 1], recv_d.at[n - 1], ds_.at[n - 1], dr.at[n - 1], chip_at(n // 2, n % 2) * 2 + core, col
            )

        def copy_t(q, c):
            return copy(
                tile.at[q], out.at[:, pl.ds(pl.multiple_of(q * 256 + c * 128, 128), 128)], ts.at[q], tr.at[q], sibling, col
            )

        def arrived(k):
            for c in range(2):
                copy(
                    mix.at[k, c], rbuf.at[k, pl.ds(c * DEPTH, DEPTH), :], rs.at[k, c], rr.at[k, c], row, mirror
                ).wait_recv()
            rt[...] = rbuf[k].T

        def product(at):
            part = jnp.dot(rt[...], hi[:, at], preferred_element_type=F32)
            return part + jnp.dot(rt[...], lo[:, at], preferred_element_type=F32)

        def multiply(k):
            arrived(k)
            for j in (2, 1, 3, 0):
                part = product(pl.ds(pl.multiple_of(lax.rem(x + j, 4) * 512, 512), 512))
                if j:
                    send_a[k, j - 1] = part.astype(BF)
                    copy_a(k, j).start()
                else:
                    own[k] = part

        def sum_x(k):
            for j in range(1, 4):
                copy_a(k, j).wait_recv()
            at_mine = pl.ds(pl.multiple_of(y * 256, 256), 256)
            at_other = pl.ds(pl.multiple_of(256 - y * 256, 256), 256)

            def total(at):
                t = own[k, :, at]
                for j in range(3):
                    t += recv_a[k, j, :, at].astype(F32)
                return t

            send_b[k] = total(at_other)
            copy_b(k).start()
            half[k] = total(at_mine)

        def pack(done, to):
            largest = jnp.max(jnp.max(jnp.abs(done), axis=0, keepdims=True), axis=1, keepdims=True)
            power = jnp.maximum(jnp.ceil(jnp.log2(jnp.maximum(largest, 1e-30))), -99.0)
            steps = jnp.clip(jnp.round(done * jnp.exp2(15.0 - power)), -32767.0, 32767.0)
            steps = steps.astype(jnp.int32).astype(jnp.int16)
            to[0:96, :] = steps[:, 0:128]
            to[96:192, :] = steps[:, 128:256]
            to[192:208, :] = jnp.broadcast_to(power, (16, 128)).astype(jnp.int32).astype(jnp.int16)

        def place(q, values):
            tile[q] = values[:, other_128].T
            copy_t(q, core).start()
            out[:, pl.ds(pl.multiple_of(q * 256 + core * 128, 128), 128)] = values[:, mine_128].T

        def spread(k, done):
            at = pl.ds(pl.multiple_of(k * 16, 16), 16)
            for q in range(8):
                gathered[q, at, :] = done[q * 16 : q * 16 + 16, :]

        def sum_y(k):
            copy_b(k).wait_recv()
            spread(k, (half[k] + recv_b[k]) * NORM)

        def step(k, carry):
            multiply(k)

            @pl.when(k >= 1)
            def _():
                sum_x(k - 1)

            @pl.when(k >= 2)
            def _():
                sum_y(k - 2)

            return carry

        lax.fori_loop(0, LAST, step, 0)
        sum_y(LAST - 2)
        for q in range(8):
            pack(gathered[q, 0:96, :], ret.at[q])

        for n in range(8):
            return_copy(lax.rem(chip + n, 8)).start()
        arrived(LAST)
        for n in (5, 4, 3, 2, 7, 6, 1, 0):
            part = product(pl.ds(pl.multiple_of(chip_at(n // 2, n % 2) * 256, 256), 256))
            if n:
                send_d[n - 1] = part.astype(BF)
                copy_d(n).start()
            else:
                half[LAST] = part
        sum_x(LAST - 1)
        total = half[LAST]
        for n in range(1, 8):
            copy_d(n).wait_recv()
            total += recv_d[n - 1].astype(F32)
        sum_y(LAST - 1)
        spread(LAST, total * NORM)
        for n in range(8):
            q = lax.rem(chip + n, 8)
            ret_last[q] = gathered[q, 96:128, :].astype(BF)
            return_last(q).start()
        for q in range(8):
            place(q, gathered.at[q])

        def finish(k, carry):
            for j in range(1, 4):
                copy_a(k, j).wait_send()
            copy_b(k).wait_send()
            return carry

        lax.fori_loop(0, LAST, finish, 0)
        for n in range(1, 8):
            copy_d(n).wait_send()
        for q in range(8):
            return_copy(q).wait_send()
            return_last(q).wait_send()
            copy_t(q, core).wait_send()
            copy_t(q, 1 - core).wait_recv()


def shards(design, species, species_weight):
    dma = pltpu.SemaphoreType.DMA
    vmem = pltpu.VMEM
    return pl.pallas_call(
        kernel,
        out_shape=jax.ShapeDtypeStruct((128, WIDTH), F32),
        in_specs=[pl.BlockSpec(memory_space=pltpu.HBM)] * 3,
        out_specs=pl.BlockSpec(memory_space=pltpu.VMEM),
        scratch_shapes=[
            vmem((2, DEPTH, WIDTH), BF),
            vmem((2, DEPTH, 128), F32),
            vmem((2 * DEPTH, WIDTH), BF),
            vmem((2 * DEPTH, WIDTH), BF),
            vmem((NB, 2 * DEPTH, 128), BF),
            vmem((128, 2 * DEPTH), BF),
            vmem((LAST, 3, 128, 512), BF),
            vmem((LAST, 3, 128, 512), BF),
            vmem((LAST, 128, 512), F32),
            vmem((LAST, 128, 256), F32),
            vmem((LAST, 128, 256), F32),
            vmem((NB, 128, 256), F32),
            vmem((8, 208, 128), jnp.int16),
            vmem((NB, 128, 128), F32),
            vmem((NB // 2, 2, DEPTH, 128), BF),
            vmem((8, 208, 128), jnp.int16),
            vmem((DEPTH,), jnp.int32),
            pltpu.SMEM((10,), F32),
            vmem((NB, 2, DEPTH, 128), BF),
            vmem((8, 128, 256), F32),
            vmem((8, 32, 256), BF),
            vmem((8, 32, 256), BF),
            vmem((7, 128, 256), BF),
            vmem((7, 128, 256), BF),
            dma((3,)),
            dma, dma, dma, dma,
            dma((NB, 2)), dma((NB, 2)),
            dma((LAST, 3)), dma((LAST, 3)),
            dma((LAST,)), dma((LAST,)),
            dma((NB,)), dma((NB,)),
            dma((8,)), dma((8,)),
            dma((NB // 2, 2)), dma((NB // 2, 2)),
            dma((7,)), dma((7,)),
            dma((8,)), dma((8,)),
        ],
        compiler_params=pltpu.CompilerParams(
            collective_id=0, has_side_effects=True, vmem_limit_bytes=50 * 2**20
        ),
        cost_estimate=pl.CostEstimate(flops=4 * 1536 * 2048 * 1024, bytes_accessed=8 * 2**20, transcendentals=0),
    )(*(pltpu.with_memory_space_constraint(a, pltpu.HBM) for a in (design, species, species_weight)))


def solution(mesh):
    placed = (P("row", "col"), P("row"), P())
    return jax.shard_map(
        shards, mesh=mesh, in_specs=placed, out_specs=P(("col", "row"), None), check_vma=False
    )
```

```python
import jax
import jax.numpy as jnp
from jax import lax
from jax.experimental import pallas as pl
from jax.experimental.pallas import tpu as pltpu
from jax.sharding import PartitionSpec as P

MESH = pl.DeviceIdType.MESH
BF = jnp.bfloat16
F32 = jnp.float32
DEPTH = 768
WIDTH = 2048
NB = 8
LAST = NB - 1
WINDOW = 2
NORM = float(12288) ** -0.5


def kernel(
    design, species, species_weight, out,
    raw, wv, hi, lo, rbuf, rt, send_a, recv_a, own, send_b, recv_b, half, ret, tile, stage, recv_q, species_here, weight_here,
    mix, gathered, ret_last, recv_l, send_d, recv_d,
    local_sem, ls, lr, ws, wr, rs, rr, as_, ar, bs, br, ts, tr, os_, orr, gs, gr, ds_, dr, fs, fr,
):
    row = lax.axis_index("row")
    col = lax.axis_index("col")
    mirror = 15 - col
    beside = lax.rem(col + 8, 16)
    core = lax.rem(row, 2)
    chip = lax.div(row, 2)
    y = lax.rem(chip, 2)
    x = lax.div(chip, 2)
    sibling = row + 1 - 2 * core
    across = row + 2 - 4 * y
    computes = lax.rem(col, 2) == 1
    barrier = pltpu.get_barrier_semaphore()

    def copy(src, dst, ss, rs_, to_row, to_col):
        return pltpu.make_async_remote_copy(
            src_ref=src, dst_ref=dst, send_sem=ss, recv_sem=rs_, device_id=(to_row, to_col), device_id_type=MESH
        )

    def greet(to_row, to_col):
        pl.semaphore_signal(barrier, inc=1, device_id=(to_row, to_col), device_id_type=MESH)

    def chip_at(j, d):
        return lax.rem(x + j, 4) * 2 + lax.rem(y + d, 2)

    mine_128 = pl.ds(pl.multiple_of(core * 128, 128), 128)
    other_128 = pl.ds(pl.multiple_of(128 - core * 128, 128), 128)
    my_rows = pl.ds(pl.multiple_of(core * DEPTH, DEPTH), DEPTH)

    def design_copy(k, c):
        return copy(mix.at[k, c], rbuf.at[k, my_rows, :], rs.at[k, c], rr.at[k, core], chip * 2 + c, mirror)

    def stage_copy(i, c):
        return copy(mix.at[2 * i + 1, c], stage.at[i, c], gs.at[i, c], gr.at[i, c], row, beside)

    def forward_copy(i, c):
        k = 2 * i + 1
        return copy(stage.at[i, c], rbuf.at[k, my_rows, :], rs.at[k, c], rr.at[k, core], chip * 2 + c, 15 - beside)

    def return_copy(q):
        return copy(ret.at[q], recv_q.at[chip], os_.at[q], orr.at[chip], 2 * q + core, mirror)

    def return_last(q):
        return copy(ret_last.at[q], recv_l.at[chip], fs.at[q], fr.at[chip], 2 * q + core, mirror)

    @pl.when(jnp.logical_not(computes))
    def _():
        for q in range(8):
            greet(2 * q + core, mirror)
        greet(row, beside)
        here = pltpu.make_async_copy(design, raw.at[0], local_sem.at[0])
        here.start()

        def mixing(k, carry):
            a = lax.broadcasted_iota(jnp.int32, (1024, 128), 0)
            b = lax.broadcasted_iota(jnp.int32, (1024, 128), 1)
            wanted = lax.div(b, 16) * 128 + k * 16 + lax.rem(b, 16)
            order = jnp.where(a == wanted, 1.0, 0.0).astype(BF)
            for c in range(2):
                found = jnp.concatenate([raw[0, :, q * 256 + c * 128 : q * 256 + c * 128 + 128] for q in range(8)], axis=1)
                mix[k, c] = jnp.dot(found, order, preferred_element_type=F32).astype(BF)
            return carry

        sends = [(k, c) for k in range(NB) for c in range(2)]

        def send(k, c):
            return forward_copy(k // 2, c) if k % 2 else design_copy(k, c)

        here.wait()
        mixing(0, 0)
        pl.semaphore_wait(barrier, 5)
        for n, (k, c) in enumerate(sends):
            if n >= WINDOW:
                send(*sends[n - WINDOW]).wait_send()
            if k % 2:
                stage_copy(k // 2, c).wait_recv()
            send(k, c).start()
            if n == 1:
                mixing(1, 0)
                for d in range(2):
                    stage_copy(0, d).start()
                lax.fori_loop(2, 4, mixing, 0)
                for d in range(2):
                    stage_copy(1, d).start()
                lax.fori_loop(4, NB, mixing, 0)
            if k in (2, 4) and c == 1:
                for d in range(2):
                    stage_copy(k // 2 + 1, d).start()
        for n in range(len(sends) - WINDOW, len(sends)):
            send(*sends[n]).wait_send()
        for i in range(NB // 2):
            for c in range(2):
                stage_copy(i, c).wait_send()
        for q in range(8):
            copy(ret.at[0], recv_q.at[q], os_.at[0], orr.at[q], row, mirror).wait_recv()
            size = jnp.exp2(recv_q[q, 192:208, :].astype(F32)[0:1, :] - 15.0)
            for h in range(2):
                at = q * 256 + h * 128
                out[0:96, at : at + 128] = recv_q[q, h * 96 : h * 96 + 96, :].astype(F32) * size
        for q in range(8):
            copy(ret_last.at[0], recv_l.at[q], fs.at[0], fr.at[q], row, mirror).wait_recv()
            out[96:128, q * 256 : q * 256 + 256] = recv_l[q].astype(F32)

    @pl.when(computes)
    def _():
        for c in range(2):
            greet(chip * 2 + c, mirror)
        for c in range(2):
            greet(chip * 2 + c, lax.rem(mirror + 8, 16))
        greet(sibling, col)
        for n in range(1, 8):
            greet(chip_at(n // 2, n % 2) * 2 + core, col)
        mine = pltpu.make_async_copy(design, raw.at[core], local_sem.at[0])
        mine.start()
        kinds = pltpu.make_async_copy(species, species_here, local_sem.at[1])
        kinds.start()
        by_kind = pltpu.make_async_copy(species_weight, weight_here, local_sem.at[2])
        by_kind.start()
        kinds.wait()
        by_kind.wait()
        for i in range(DEPTH // 128):
            kind = species_here[i * 128 : i * 128 + 128].reshape(1, 128)
            value = jnp.zeros((1, 128), F32)
            for n in range(10):
                value = jnp.where(kind == n, weight_here[n], value)
            wv[core, i * 128 : i * 128 + 128, :] = jnp.broadcast_to(value, (128, 128)).T
        pl.semaphore_wait(barrier, 16)
        theirs = copy(design, raw.at[core], ls, lr, sibling, col)
        theirs_w = copy(wv.at[core], wv.at[core], ws, wr, sibling, col)
        theirs_w.start()
        theirs.start()

        def scale(s):
            def some(i, carry):
                at = pl.ds(pl.multiple_of(i * 32, 32), 32)
                to = pl.ds(pl.multiple_of(s * DEPTH + i * 32, 32), 32)
                value = raw[s, at, :].astype(F32) * wv[s, at, 0:1]
                high = value.astype(BF)
                hi[to, :] = high
                lo[to, :] = (value - high.astype(F32)).astype(BF)
                return carry

            lax.fori_loop(0, DEPTH // 32, some, 0)

        mine.wait()
        scale(core)
        theirs_w.wait()
        theirs.wait()
        scale(1 - core)

        def copy_a(k, j):
            return copy(
                send_a.at[k, j - 1], recv_a.at[k, j - 1], as_.at[k, j - 1], ar.at[k, j - 1], chip_at(j, 0) * 2 + core, col
            )

        def copy_b(k):
            return copy(send_b.at[k], recv_b.at[k], bs.at[k], br.at[k], across, col)

        def copy_d(n):
            return copy(
                send_d.at[n - 1], recv_d.at[n - 1], ds_.at[n - 1], dr.at[n - 1], chip_at(n // 2, n % 2) * 2 + core, col
            )

        def copy_t(q, c):
            return copy(
                tile.at[q], out.at[:, pl.ds(pl.multiple_of(q * 256 + c * 128, 128), 128)], ts.at[q], tr.at[q], sibling, col
            )

        def arrived(k):
            for c in range(2):
                copy(
                    mix.at[k, c], rbuf.at[k, pl.ds(c * DEPTH, DEPTH), :], rs.at[k, c], rr.at[k, c], row, mirror
                ).wait_recv()
            rt[...] = rbuf[k].T

        def product(at):
            part = jnp.dot(rt[...], hi[:, at], preferred_element_type=F32)
            return part + jnp.dot(rt[...], lo[:, at], preferred_element_type=F32)

        def multiply(k):
            arrived(k)
            for j in (2, 1, 3, 0):
                part = product(pl.ds(pl.multiple_of(lax.rem(x + j, 4) * 512, 512), 512))
                if j:
                    send_a[k, j - 1] = part.astype(BF)
                    copy_a(k, j).start()
                else:
                    own[k] = part

        def sum_x(k):
            for j in range(1, 4):
                copy_a(k, j).wait_recv()
            at_mine = pl.ds(pl.multiple_of(y * 256, 256), 256)
            at_other = pl.ds(pl.multiple_of(256 - y * 256, 256), 256)

            def total(at):
                t = own[k, :, at]
                for j in range(3):
                    t += recv_a[k, j, :, at].astype(F32)
                return t

            send_b[k] = total(at_other)
            copy_b(k).start()
            half[k] = total(at_mine)

        def pack(done, to):
            largest = jnp.max(jnp.max(jnp.abs(done), axis=0, keepdims=True), axis=1, keepdims=True)
            power = jnp.maximum(jnp.ceil(jnp.log2(jnp.maximum(largest, 1e-30))), -99.0)
            steps = jnp.clip(jnp.round(done * jnp.exp2(15.0 - power)), -32767.0, 32767.0)
            steps = steps.astype(jnp.int32).astype(jnp.int16)
            to[0:96, :] = steps[:, 0:128]
            to[96:192, :] = steps[:, 128:256]
            to[192:208, :] = jnp.broadcast_to(power, (16, 128)).astype(jnp.int32).astype(jnp.int16)

        def place(q, values):
            tile[q] = values[:, other_128].T
            copy_t(q, core).start()
            out[:, pl.ds(pl.multiple_of(q * 256 + core * 128, 128), 128)] = values[:, mine_128].T

        def spread(k, done):
            at = pl.ds(pl.multiple_of(k * 16, 16), 16)
            for q in range(8):
                gathered[q, at, :] = done[q * 16 : q * 16 + 16, :]

        def sum_y(k):
            copy_b(k).wait_recv()
            spread(k, (half[k] + recv_b[k]) * NORM)

        def step(k, carry):
            multiply(k)

            @pl.when(k >= 1)
            def _():
                sum_x(k - 1)

            @pl.when(k >= 2)
            def _():
                sum_y(k - 2)

            return carry

        lax.fori_loop(0, LAST, step, 0)
        sum_y(LAST - 2)
        for q in range(8):
            pack(gathered[q, 0:96, :], ret.at[q])

        for n in range(8):
            return_copy(lax.rem(chip + n, 8)).start()
        sum_x(LAST - 1)
        arrived(LAST)
        for n in (5, 4, 3, 2, 7, 6, 1, 0):
            part = product(pl.ds(pl.multiple_of(chip_at(n // 2, n % 2) * 256, 256), 256))
            if n:
                send_d[n - 1] = part.astype(BF)
                copy_d(n).start()
            else:
                half[LAST] = part
        sum_y(LAST - 1)
        total = half[LAST]
        for n in range(1, 8):
            copy_d(n).wait_recv()
            total += recv_d[n - 1].astype(F32)
        spread(LAST, total * NORM)
        for n in range(8):
            q = lax.rem(chip + n, 8)
            ret_last[q] = gathered[q, 96:128, :].astype(BF)
            return_last(q).start()
        for q in range(8):
            place(q, gathered.at[q])

        def finish(k, carry):
            for j in range(1, 4):
                copy_a(k, j).wait_send()
            copy_b(k).wait_send()
            return carry

        lax.fori_loop(0, LAST, finish, 0)
        for n in range(1, 8):
            copy_d(n).wait_send()
        for q in range(8):
            return_copy(q).wait_send()
            return_last(q).wait_send()
            copy_t(q, core).wait_send()
            copy_t(q, 1 - core).wait_recv()


def shards(design, species, species_weight):
    dma = pltpu.SemaphoreType.DMA
    vmem = pltpu.VMEM
    return pl.pallas_call(
        kernel,
        out_shape=jax.ShapeDtypeStruct((128, WIDTH), F32),
        in_specs=[pl.BlockSpec(memory_space=pltpu.HBM)] * 3,
        out_specs=pl.BlockSpec(memory_space=pltpu.VMEM),
        scratch_shapes=[
            vmem((2, DEPTH, WIDTH), BF),
            vmem((2, DEPTH, 128), F32),
            vmem((2 * DEPTH, WIDTH), BF),
            vmem((2 * DEPTH, WIDTH), BF),
            vmem((NB, 2 * DEPTH, 128), BF),
            vmem((128, 2 * DEPTH), BF),
            vmem((LAST, 3, 128, 512), BF),
            vmem((LAST, 3, 128, 512), BF),
            vmem((LAST, 128, 512), F32),
            vmem((LAST, 128, 256), F32),
            vmem((LAST, 128, 256), F32),
            vmem((NB, 128, 256), F32),
            vmem((8, 208, 128), jnp.int16),
            vmem((NB, 128, 128), F32),
            vmem((NB // 2, 2, DEPTH, 128), BF),
            vmem((8, 208, 128), jnp.int16),
            vmem((DEPTH,), jnp.int32),
            pltpu.SMEM((10,), F32),
            vmem((NB, 2, DEPTH, 128), BF),
            vmem((8, 128, 256), F32),
            vmem((8, 32, 256), BF),
            vmem((8, 32, 256), BF),
            vmem((7, 128, 256), BF),
            vmem((7, 128, 256), BF),
            dma((3,)),
            dma, dma, dma, dma,
            dma((NB, 2)), dma((NB, 2)),
            dma((LAST, 3)), dma((LAST, 3)),
            dma((LAST,)), dma((LAST,)),
            dma((NB,)), dma((NB,)),
            dma((8,)), dma((8,)),
            dma((NB // 2, 2)), dma((NB // 2, 2)),
            dma((7,)), dma((7,)),
            dma((8,)), dma((8,)),
        ],
        compiler_params=pltpu.CompilerParams(
            collective_id=0, has_side_effects=True, vmem_limit_bytes=50 * 2**20
        ),
        cost_estimate=pl.CostEstimate(flops=4 * 1536 * 2048 * 1024, bytes_accessed=8 * 2**20, transcendentals=0),
    )(*(pltpu.with_memory_space_constraint(a, pltpu.HBM) for a in (design, species, species_weight)))


def solution(mesh):
    placed = (P("row", "col"), P("row"), P())
    return jax.shard_map(
        shards, mesh=mesh, in_specs=placed, out_specs=P(("col", "row"), None), check_vma=False
    )
```

```python
import jax
import jax.numpy as jnp
from jax import lax
from jax.experimental import pallas as pl
from jax.experimental.pallas import tpu as pltpu
from jax.sharding import PartitionSpec as P

MESH = pl.DeviceIdType.MESH
BF = jnp.bfloat16
F32 = jnp.float32
DEPTH = 768
WIDTH = 2048
NB = 8
LAST = NB - 1
WINDOW = 2
NORM = float(12288) ** -0.5


def kernel(
    design, species, species_weight, out,
    raw, wv, hi, lo, rbuf, rt, send_a, recv_a, own, send_b, recv_b, half, ret, tile, stage, recv_q, species_here, weight_here,
    mix, gathered, ret_last, recv_l, send_d, recv_d,
    local_sem, ls, lr, ws, wr, rs, rr, as_, ar, bs, br, ts, tr, os_, orr, gs, gr, ds_, dr, fs, fr,
):
    row = lax.axis_index("row")
    col = lax.axis_index("col")
    mirror = 15 - col
    beside = lax.rem(col + 8, 16)
    core = lax.rem(row, 2)
    chip = lax.div(row, 2)
    y = lax.rem(chip, 2)
    x = lax.div(chip, 2)
    sibling = row + 1 - 2 * core
    across = row + 2 - 4 * y
    computes = lax.rem(col, 2) == 1
    barrier = pltpu.get_barrier_semaphore()

    def copy(src, dst, ss, rs_, to_row, to_col):
        return pltpu.make_async_remote_copy(
            src_ref=src, dst_ref=dst, send_sem=ss, recv_sem=rs_, device_id=(to_row, to_col), device_id_type=MESH
        )

    def greet(to_row, to_col):
        pl.semaphore_signal(barrier, inc=1, device_id=(to_row, to_col), device_id_type=MESH)

    def chip_at(j, d):
        return lax.rem(x + j, 4) * 2 + lax.rem(y + d, 2)

    mine_128 = pl.ds(pl.multiple_of(core * 128, 128), 128)
    other_128 = pl.ds(pl.multiple_of(128 - core * 128, 128), 128)
    my_rows = pl.ds(pl.multiple_of(core * DEPTH, DEPTH), DEPTH)

    def design_copy(k, c):
        return copy(mix.at[k, c], rbuf.at[k, my_rows, :], rs.at[k, c], rr.at[k, core], chip * 2 + c, mirror)

    def stage_copy(i, c):
        return copy(mix.at[2 * i + 1, c], stage.at[i, c], gs.at[i, c], gr.at[i, c], row, beside)

    def forward_copy(i, c):
        k = 2 * i + 1
        return copy(stage.at[i, c], rbuf.at[k, my_rows, :], rs.at[k, c], rr.at[k, core], chip * 2 + c, 15 - beside)

    def return_copy(q):
        return copy(ret.at[q], recv_q.at[chip], os_.at[q], orr.at[chip], 2 * q + core, mirror)

    def return_last(q, h):
        rows = pl.ds(16 * h, 16)
        return copy(ret_last.at[q, rows, :], recv_l.at[chip, rows, :], fs.at[q, h], fr.at[chip, h], 2 * q + core, mirror)

    @pl.when(jnp.logical_not(computes))
    def _():
        for q in range(8):
            greet(2 * q + core, mirror)
        greet(row, beside)
        here = pltpu.make_async_copy(design, raw.at[0], local_sem.at[0])
        here.start()

        def mixing(k, carry):
            a = lax.broadcasted_iota(jnp.int32, (1024, 128), 0)
            b = lax.broadcasted_iota(jnp.int32, (1024, 128), 1)
            wanted = lax.div(b, 16) * 128 + k * 16 + lax.rem(b, 16)
            order = jnp.where(a == wanted, 1.0, 0.0).astype(BF)
            for c in range(2):
                found = jnp.concatenate([raw[0, :, q * 256 + c * 128 : q * 256 + c * 128 + 128] for q in range(8)], axis=1)
                mix[k, c] = jnp.dot(found, order, preferred_element_type=F32).astype(BF)
            return carry

        sends = [(k, c) for k in range(NB) for c in range(2)]

        def send(k, c):
            return forward_copy(k // 2, c) if k % 2 else design_copy(k, c)

        here.wait()
        mixing(0, 0)
        pl.semaphore_wait(barrier, 5)
        for n, (k, c) in enumerate(sends):
            if n >= WINDOW:
                send(*sends[n - WINDOW]).wait_send()
            if k % 2:
                stage_copy(k // 2, c).wait_recv()
            send(k, c).start()
            if n == 1:
                mixing(1, 0)
                for d in range(2):
                    stage_copy(0, d).start()
                lax.fori_loop(2, 4, mixing, 0)
                for d in range(2):
                    stage_copy(1, d).start()
                lax.fori_loop(4, NB, mixing, 0)
            if k in (2, 4) and c == 1:
                for d in range(2):
                    stage_copy(k // 2 + 1, d).start()
        for n in range(len(sends) - WINDOW, len(sends)):
            send(*sends[n]).wait_send()
        for i in range(NB // 2):
            for c in range(2):
                stage_copy(i, c).wait_send()
        for q in range(8):
            copy(ret.at[0], recv_q.at[q], os_.at[0], orr.at[q], row, mirror).wait_recv()
            size = jnp.exp2(recv_q[q, 192:208, :].astype(F32)[0:1, :] - 15.0)
            for h in range(2):
                at = q * 256 + h * 128
                out[0:96, at : at + 128] = recv_q[q, h * 96 : h * 96 + 96, :].astype(F32) * size
        for q in range(8):
            for h in range(2):
                rows = pl.ds(16 * h, 16)
                copy(ret_last.at[0, rows, :], recv_l.at[q, rows, :], fs.at[0, h], fr.at[q, h], row, mirror).wait_recv()
            out[96:128, q * 256 : q * 256 + 256] = recv_l[q].astype(F32)

    @pl.when(computes)
    def _():
        for c in range(2):
            greet(chip * 2 + c, mirror)
        for c in range(2):
            greet(chip * 2 + c, lax.rem(mirror + 8, 16))
        greet(sibling, col)
        for n in range(1, 8):
            greet(chip_at(n // 2, n % 2) * 2 + core, col)
        mine = pltpu.make_async_copy(design, raw.at[core], local_sem.at[0])
        mine.start()
        kinds = pltpu.make_async_copy(species, species_here, local_sem.at[1])
        kinds.start()
        by_kind = pltpu.make_async_copy(species_weight, weight_here, local_sem.at[2])
        by_kind.start()
        kinds.wait()
        by_kind.wait()
        for i in range(DEPTH // 128):
            kind = species_here[i * 128 : i * 128 + 128].reshape(1, 128)
            value = jnp.zeros((1, 128), F32)
            for n in range(10):
                value = jnp.where(kind == n, weight_here[n], value)
            wv[core, i * 128 : i * 128 + 128, :] = jnp.broadcast_to(value, (128, 128)).T
        pl.semaphore_wait(barrier, 16)
        theirs = copy(design, raw.at[core], ls, lr, sibling, col)
        theirs_w = copy(wv.at[core], wv.at[core], ws, wr, sibling, col)
        theirs_w.start()
        theirs.start()

        def scale(s):
            def some(i, carry):
                at = pl.ds(pl.multiple_of(i * 32, 32), 32)
                to = pl.ds(pl.multiple_of(s * DEPTH + i * 32, 32), 32)
                value = raw[s, at, :].astype(F32) * wv[s, at, 0:1]
                high = value.astype(BF)
                hi[to, :] = high
                lo[to, :] = (value - high.astype(F32)).astype(BF)
                return carry

            lax.fori_loop(0, DEPTH // 32, some, 0)

        mine.wait()
        scale(core)
        theirs_w.wait()
        theirs.wait()
        scale(1 - core)

        def copy_a(k, j):
            return copy(
                send_a.at[k, j - 1], recv_a.at[k, j - 1], as_.at[k, j - 1], ar.at[k, j - 1], chip_at(j, 0) * 2 + core, col
            )

        def copy_b(k):
            return copy(send_b.at[k], recv_b.at[k], bs.at[k], br.at[k], across, col)

        def copy_d(n):
            return copy(
                send_d.at[n - 1], recv_d.at[n - 1], ds_.at[n - 1], dr.at[n - 1], chip_at(n // 2, n % 2) * 2 + core, col
            )

        def copy_t(q, c):
            return copy(
                tile.at[q], out.at[:, pl.ds(pl.multiple_of(q * 256 + c * 128, 128), 128)], ts.at[q], tr.at[q], sibling, col
            )

        def arrived(k):
            for c in range(2):
                copy(
                    mix.at[k, c], rbuf.at[k, pl.ds(c * DEPTH, DEPTH), :], rs.at[k, c], rr.at[k, c], row, mirror
                ).wait_recv()
            rt[...] = rbuf[k].T

        def product(at):
            part = jnp.dot(rt[...], hi[:, at], preferred_element_type=F32)
            return part + jnp.dot(rt[...], lo[:, at], preferred_element_type=F32)

        def multiply(k):
            arrived(k)
            for j in (2, 1, 3, 0):
                part = product(pl.ds(pl.multiple_of(lax.rem(x + j, 4) * 512, 512), 512))
                if j:
                    send_a[k, j - 1] = part.astype(BF)
                    copy_a(k, j).start()
                else:
                    own[k] = part

        def sum_x(k):
            for j in range(1, 4):
                copy_a(k, j).wait_recv()
            at_mine = pl.ds(pl.multiple_of(y * 256, 256), 256)
            at_other = pl.ds(pl.multiple_of(256 - y * 256, 256), 256)

            def total(at):
                t = own[k, :, at]
                for j in range(3):
                    t += recv_a[k, j, :, at].astype(F32)
                return t

            send_b[k] = total(at_other)
            copy_b(k).start()
            half[k] = total(at_mine)

        def pack(done, to):
            largest = jnp.max(jnp.max(jnp.abs(done), axis=0, keepdims=True), axis=1, keepdims=True)
            power = jnp.maximum(jnp.ceil(jnp.log2(jnp.maximum(largest, 1e-30))), -99.0)
            steps = jnp.clip(jnp.round(done * jnp.exp2(15.0 - power)), -32767.0, 32767.0)
            steps = steps.astype(jnp.int32).astype(jnp.int16)
            to[0:96, :] = steps[:, 0:128]
            to[96:192, :] = steps[:, 128:256]
            to[192:208, :] = jnp.broadcast_to(power, (16, 128)).astype(jnp.int32).astype(jnp.int16)

        def place(q, values):
            tile[q] = values[:, other_128].T
            copy_t(q, core).start()
            out[:, pl.ds(pl.multiple_of(q * 256 + core * 128, 128), 128)] = values[:, mine_128].T

        def spread(k, done):
            at = pl.ds(pl.multiple_of(k * 16, 16), 16)
            for q in range(8):
                gathered[q, at, :] = done[q * 16 : q * 16 + 16, :]

        def sum_y(k):
            copy_b(k).wait_recv()
            spread(k, (half[k] + recv_b[k]) * NORM)

        def step(k, carry):
            multiply(k)

            @pl.when(k >= 1)
            def _():
                sum_x(k - 1)

            @pl.when(k >= 2)
            def _():
                sum_y(k - 2)

            return carry

        lax.fori_loop(0, LAST, step, 0)
        sum_y(LAST - 2)
        for q in range(8):
            pack(gathered[q, 0:96, :], ret.at[q])

        for n in range(8):
            return_copy(lax.rem(chip + n, 8)).start()
        sum_x(LAST - 1)
        arrived(LAST)
        for n in (5, 4, 3, 2, 7, 6, 1, 0):
            part = product(pl.ds(pl.multiple_of(chip_at(n // 2, n % 2) * 256, 256), 256))
            if n:
                send_d[n - 1] = part.astype(BF)
                copy_d(n).start()
            else:
                half[LAST] = part
        sum_y(LAST - 1)
        for n in range(8):
            q = lax.rem(chip + n, 8)
            ret_last[q, 0:16, :] = gathered[q, 96:112, :].astype(BF)
            return_last(q, 0).start()
        total = half[LAST]
        for n in range(1, 8):
            copy_d(n).wait_recv()
            total += recv_d[n - 1].astype(F32)
        spread(LAST, total * NORM)
        for n in range(8):
            q = lax.rem(chip + n, 8)
            ret_last[q, 16:32, :] = gathered[q, 112:128, :].astype(BF)
            return_last(q, 1).start()
        for q in range(8):
            place(q, gathered.at[q])

        def finish(k, carry):
            for j in range(1, 4):
                copy_a(k, j).wait_send()
            copy_b(k).wait_send()
            return carry

        lax.fori_loop(0, LAST, finish, 0)
        for n in range(1, 8):
            copy_d(n).wait_send()
        for q in range(8):
            return_copy(q).wait_send()
            return_last(q, 0).wait_send()
            return_last(q, 1).wait_send()
            copy_t(q, core).wait_send()
            copy_t(q, 1 - core).wait_recv()


def shards(design, species, species_weight):
    dma = pltpu.SemaphoreType.DMA
    vmem = pltpu.VMEM
    return pl.pallas_call(
        kernel,
        out_shape=jax.ShapeDtypeStruct((128, WIDTH), F32),
        in_specs=[pl.BlockSpec(memory_space=pltpu.HBM)] * 3,
        out_specs=pl.BlockSpec(memory_space=pltpu.VMEM),
        scratch_shapes=[
            vmem((2, DEPTH, WIDTH), BF),
            vmem((2, DEPTH, 128), F32),
            vmem((2 * DEPTH, WIDTH), BF),
            vmem((2 * DEPTH, WIDTH), BF),
            vmem((NB, 2 * DEPTH, 128), BF),
            vmem((128, 2 * DEPTH), BF),
            vmem((LAST, 3, 128, 512), BF),
            vmem((LAST, 3, 128, 512), BF),
            vmem((LAST, 128, 512), F32),
            vmem((LAST, 128, 256), F32),
            vmem((LAST, 128, 256), F32),
            vmem((NB, 128, 256), F32),
            vmem((8, 208, 128), jnp.int16),
            vmem((NB, 128, 128), F32),
            vmem((NB // 2, 2, DEPTH, 128), BF),
            vmem((8, 208, 128), jnp.int16),
            vmem((DEPTH,), jnp.int32),
            pltpu.SMEM((10,), F32),
            vmem((NB, 2, DEPTH, 128), BF),
            vmem((8, 128, 256), F32),
            vmem((8, 32, 256), BF),
            vmem((8, 32, 256), BF),
            vmem((7, 128, 256), BF),
            vmem((7, 128, 256), BF),
            dma((3,)),
            dma, dma, dma, dma,
            dma((NB, 2)), dma((NB, 2)),
            dma((LAST, 3)), dma((LAST, 3)),
            dma((LAST,)), dma((LAST,)),
            dma((NB,)), dma((NB,)),
            dma((8,)), dma((8,)),
            dma((NB // 2, 2)), dma((NB // 2, 2)),
            dma((7,)), dma((7,)),
            dma((8, 2)), dma((8, 2)),
        ],
        compiler_params=pltpu.CompilerParams(
            collective_id=0, has_side_effects=True, vmem_limit_bytes=50 * 2**20
        ),
        cost_estimate=pl.CostEstimate(flops=4 * 1536 * 2048 * 1024, bytes_accessed=8 * 2**20, transcendentals=0),
    )(*(pltpu.with_memory_space_constraint(a, pltpu.HBM) for a in (design, species, species_weight)))


def solution(mesh):
    placed = (P("row", "col"), P("row"), P())
    return jax.shard_map(
        shards, mesh=mesh, in_specs=placed, out_specs=P(("col", "row"), None), check_vma=False
    )
```

```python
import jax
import jax.numpy as jnp
from jax import lax
from jax.experimental import pallas as pl
from jax.experimental.pallas import tpu as pltpu
from jax.sharding import PartitionSpec as P

MESH = pl.DeviceIdType.MESH
BF = jnp.bfloat16
F32 = jnp.float32
DEPTH = 768
WIDTH = 2048
NB = 8
LAST = NB - 1
WINDOW = 2
NORM = float(12288) ** -0.5


def kernel(
    design, species, species_weight, out,
    raw, wv, hi, lo, rbuf, rt, send_a, recv_a, own, send_b, recv_b, half, ret, tile, stage, recv_q, species_here, weight_here,
    mix, gathered, ret_last, recv_l, send_d, recv_d,
    local_sem, ls, lr, ws, wr, rs, rr, as_, ar, bs, br, ts, tr, os_, orr, gs, gr, ds_, dr, fs, fr,
):
    row = lax.axis_index("row")
    col = lax.axis_index("col")
    mirror = 15 - col
    beside = lax.rem(col + 8, 16)
    core = lax.rem(row, 2)
    chip = lax.div(row, 2)
    y = lax.rem(chip, 2)
    x = lax.div(chip, 2)
    sibling = row + 1 - 2 * core
    across = row + 2 - 4 * y
    computes = lax.rem(col, 2) == 1
    barrier = pltpu.get_barrier_semaphore()

    def copy(src, dst, ss, rs_, to_row, to_col):
        return pltpu.make_async_remote_copy(
            src_ref=src, dst_ref=dst, send_sem=ss, recv_sem=rs_, device_id=(to_row, to_col), device_id_type=MESH
        )

    def greet(to_row, to_col):
        pl.semaphore_signal(barrier, inc=1, device_id=(to_row, to_col), device_id_type=MESH)

    def chip_at(j, d):
        return lax.rem(x + j, 4) * 2 + lax.rem(y + d, 2)

    mine_128 = pl.ds(pl.multiple_of(core * 128, 128), 128)
    other_128 = pl.ds(pl.multiple_of(128 - core * 128, 128), 128)
    my_rows = pl.ds(pl.multiple_of(core * DEPTH, DEPTH), DEPTH)

    def design_copy(k, c):
        return copy(mix.at[k, c], rbuf.at[k, my_rows, :], rs.at[k, c], rr.at[k, core], chip * 2 + c, mirror)

    def stage_copy(i, c):
        return copy(mix.at[2 * i + 1, c], stage.at[i, c], gs.at[i, c], gr.at[i, c], row, beside)

    def forward_copy(i, c):
        k = 2 * i + 1
        return copy(stage.at[i, c], rbuf.at[k, my_rows, :], rs.at[k, c], rr.at[k, core], chip * 2 + c, 15 - beside)

    def return_copy(q):
        return copy(ret.at[q], recv_q.at[chip], os_.at[q], orr.at[chip], 2 * q + core, mirror)

    def return_last(q, h):
        rows = pl.ds(16 * h, 16)
        return copy(ret_last.at[q, rows, :], recv_l.at[chip, rows, :], fs.at[q, h], fr.at[chip, h], 2 * q + core, mirror)

    @pl.when(jnp.logical_not(computes))
    def _():
        for q in range(8):
            greet(2 * q + core, mirror)
        greet(row, beside)
        here = pltpu.make_async_copy(design, raw.at[0], local_sem.at[0])
        here.start()

        def order_of(k):
            a = lax.broadcasted_iota(jnp.int32, (1024, 128), 0)
            b = lax.broadcasted_iota(jnp.int32, (1024, 128), 1)
            wanted = lax.div(b, 16) * 128 + k * 16 + lax.rem(b, 16)
            return jnp.where(a == wanted, 1.0, 0.0).astype(BF)

        def mix_columns(k, order):
            for c in range(2):
                found = jnp.concatenate([raw[0, :, q * 256 + c * 128 : q * 256 + c * 128 + 128] for q in range(8)], axis=1)
                mix[k, c] = jnp.dot(found, order, preferred_element_type=F32).astype(BF)

        def mixing(k, carry):
            mix_columns(k, order_of(k))
            return carry

        sends = [(k, c) for k in range(NB) for c in range(2)]

        def send(k, c):
            return forward_copy(k // 2, c) if k % 2 else design_copy(k, c)

        first = order_of(0)
        here.wait()
        mix_columns(0, first)
        pl.semaphore_wait(barrier, 5)
        for n, (k, c) in enumerate(sends):
            if n >= WINDOW:
                send(*sends[n - WINDOW]).wait_send()
            if k % 2:
                stage_copy(k // 2, c).wait_recv()
            send(k, c).start()
            if n == 1:
                mixing(1, 0)
                for d in range(2):
                    stage_copy(0, d).start()
                lax.fori_loop(2, 4, mixing, 0)
                for d in range(2):
                    stage_copy(1, d).start()
                lax.fori_loop(4, NB, mixing, 0)
            if k in (2, 4) and c == 1:
                for d in range(2):
                    stage_copy(k // 2 + 1, d).start()
        for n in range(len(sends) - WINDOW, len(sends)):
            send(*sends[n]).wait_send()
        for i in range(NB // 2):
            for c in range(2):
                stage_copy(i, c).wait_send()
        for q in range(8):
            copy(ret.at[0], recv_q.at[q], os_.at[0], orr.at[q], row, mirror).wait_recv()
            size = jnp.exp2(recv_q[q, 192:208, :].astype(F32)[0:1, :] - 15.0)
            for h in range(2):
                at = q * 256 + h * 128
                out[0:96, at : at + 128] = recv_q[q, h * 96 : h * 96 + 96, :].astype(F32) * size
        for q in range(8):
            for h in range(2):
                rows = pl.ds(16 * h, 16)
                copy(ret_last.at[0, rows, :], recv_l.at[q, rows, :], fs.at[0, h], fr.at[q, h], row, mirror).wait_recv()
            out[96:128, q * 256 : q * 256 + 256] = recv_l[q].astype(F32)

    @pl.when(computes)
    def _():
        for c in range(2):
            greet(chip * 2 + c, mirror)
        for c in range(2):
            greet(chip * 2 + c, lax.rem(mirror + 8, 16))
        greet(sibling, col)
        for n in range(1, 8):
            greet(chip_at(n // 2, n % 2) * 2 + core, col)
        mine = pltpu.make_async_copy(design, raw.at[core], local_sem.at[0])
        mine.start()
        kinds = pltpu.make_async_copy(species, species_here, local_sem.at[1])
        kinds.start()
        by_kind = pltpu.make_async_copy(species_weight, weight_here, local_sem.at[2])
        by_kind.start()
        kinds.wait()
        by_kind.wait()
        for i in range(DEPTH // 128):
            kind = species_here[i * 128 : i * 128 + 128].reshape(1, 128)
            value = jnp.zeros((1, 128), F32)
            for n in range(10):
                value = jnp.where(kind == n, weight_here[n], value)
            wv[core, i * 128 : i * 128 + 128, :] = jnp.broadcast_to(value, (128, 128)).T
        pl.semaphore_wait(barrier, 16)
        theirs = copy(design, raw.at[core], ls, lr, sibling, col)
        theirs_w = copy(wv.at[core], wv.at[core], ws, wr, sibling, col)
        theirs_w.start()
        theirs.start()

        def scale(s):
            def some(i, carry):
                at = pl.ds(pl.multiple_of(i * 32, 32), 32)
                to = pl.ds(pl.multiple_of(s * DEPTH + i * 32, 32), 32)
                value = raw[s, at, :].astype(F32) * wv[s, at, 0:1]
                high = value.astype(BF)
                hi[to, :] = high
                lo[to, :] = (value - high.astype(F32)).astype(BF)
                return carry

            lax.fori_loop(0, DEPTH // 32, some, 0)

        mine.wait()
        scale(core)
        theirs_w.wait()
        theirs.wait()
        scale(1 - core)

        def copy_a(k, j):
            return copy(
                send_a.at[k, j - 1], recv_a.at[k, j - 1], as_.at[k, j - 1], ar.at[k, j - 1], chip_at(j, 0) * 2 + core, col
            )

        def copy_b(k):
            return copy(send_b.at[k], recv_b.at[k], bs.at[k], br.at[k], across, col)

        def copy_d(n):
            return copy(
                send_d.at[n - 1], recv_d.at[n - 1], ds_.at[n - 1], dr.at[n - 1], chip_at(n // 2, n % 2) * 2 + core, col
            )

        def copy_t(q, c):
            return copy(
                tile.at[q], out.at[:, pl.ds(pl.multiple_of(q * 256 + c * 128, 128), 128)], ts.at[q], tr.at[q], sibling, col
            )

        def arrived(k):
            for c in range(2):
                copy(
                    mix.at[k, c], rbuf.at[k, pl.ds(c * DEPTH, DEPTH), :], rs.at[k, c], rr.at[k, c], row, mirror
                ).wait_recv()
            rt[...] = rbuf[k].T

        def product(at):
            part = jnp.dot(rt[...], hi[:, at], preferred_element_type=F32)
            return part + jnp.dot(rt[...], lo[:, at], preferred_element_type=F32)

        def multiply(k):
            arrived(k)
            for j in (2, 1, 3, 0):
                part = product(pl.ds(pl.multiple_of(lax.rem(x + j, 4) * 512, 512), 512))
                if j:
                    send_a[k, j - 1] = part.astype(BF)
                    copy_a(k, j).start()
                else:
                    own[k] = part

        def sum_x(k):
            for j in range(1, 4):
                copy_a(k, j).wait_recv()
            at_mine = pl.ds(pl.multiple_of(y * 256, 256), 256)
            at_other = pl.ds(pl.multiple_of(256 - y * 256, 256), 256)

            def total(at):
                t = own[k, :, at]
                for j in range(3):
                    t += recv_a[k, j, :, at].astype(F32)
                return t

            send_b[k] = total(at_other)
            copy_b(k).start()
            half[k] = total(at_mine)

        def pack(done, to):
            largest = jnp.max(jnp.max(jnp.abs(done), axis=0, keepdims=True), axis=1, keepdims=True)
            power = jnp.maximum(jnp.ceil(jnp.log2(jnp.maximum(largest, 1e-30))), -99.0)
            steps = jnp.clip(jnp.round(done * jnp.exp2(15.0 - power)), -32767.0, 32767.0)
            steps = steps.astype(jnp.int32).astype(jnp.int16)
            to[0:96, :] = steps[:, 0:128]
            to[96:192, :] = steps[:, 128:256]
            to[192:208, :] = jnp.broadcast_to(power, (16, 128)).astype(jnp.int32).astype(jnp.int16)

        def place(q, values):
            tile[q] = values[:, other_128].T
            copy_t(q, core).start()
            out[:, pl.ds(pl.multiple_of(q * 256 + core * 128, 128), 128)] = values[:, mine_128].T

        def spread(k, done):
            at = pl.ds(pl.multiple_of(k * 16, 16), 16)
            for q in range(8):
                gathered[q, at, :] = done[q * 16 : q * 16 + 16, :]

        def sum_y(k):
            copy_b(k).wait_recv()
            spread(k, (half[k] + recv_b[k]) * NORM)

        def step(k, carry):
            multiply(k)

            @pl.when(k >= 1)
            def _():
                sum_x(k - 1)

            @pl.when(k >= 2)
            def _():
                sum_y(k - 2)

            return carry

        lax.fori_loop(0, LAST, step, 0)
        sum_y(LAST - 2)
        for q in range(8):
            pack(gathered[q, 0:96, :], ret.at[q])

        for n in range(8):
            return_copy(lax.rem(chip + n, 8)).start()
        sum_x(LAST - 1)
        arrived(LAST)
        for n in (5, 4, 3, 2, 7, 6, 1, 0):
            part = product(pl.ds(pl.multiple_of(chip_at(n // 2, n % 2) * 256, 256), 256))
            if n:
                send_d[n - 1] = part.astype(BF)
                copy_d(n).start()
            else:
                half[LAST] = part
        sum_y(LAST - 1)
        for n in range(8):
            q = lax.rem(chip + n, 8)
            ret_last[q, 0:16, :] = gathered[q, 96:112, :].astype(BF)
            return_last(q, 0).start()
        total = half[LAST]
        for n in range(1, 8):
            copy_d(n).wait_recv()
            total += recv_d[n - 1].astype(F32)
        spread(LAST, total * NORM)
        for n in range(8):
            q = lax.rem(chip + n, 8)
            ret_last[q, 16:32, :] = gathered[q, 112:128, :].astype(BF)
            return_last(q, 1).start()
        for q in range(8):
            place(q, gathered.at[q])

        def finish(k, carry):
            for j in range(1, 4):
                copy_a(k, j).wait_send()
            copy_b(k).wait_send()
            return carry

        lax.fori_loop(0, LAST, finish, 0)
        for n in range(1, 8):
            copy_d(n).wait_send()
        for q in range(8):
            return_copy(q).wait_send()
            return_last(q, 0).wait_send()
            return_last(q, 1).wait_send()
            copy_t(q, core).wait_send()
            copy_t(q, 1 - core).wait_recv()


def shards(design, species, species_weight):
    dma = pltpu.SemaphoreType.DMA
    vmem = pltpu.VMEM
    return pl.pallas_call(
        kernel,
        out_shape=jax.ShapeDtypeStruct((128, WIDTH), F32),
        in_specs=[pl.BlockSpec(memory_space=pltpu.HBM)] * 3,
        out_specs=pl.BlockSpec(memory_space=pltpu.VMEM),
        scratch_shapes=[
            vmem((2, DEPTH, WIDTH), BF),
            vmem((2, DEPTH, 128), F32),
            vmem((2 * DEPTH, WIDTH), BF),
            vmem((2 * DEPTH, WIDTH), BF),
            vmem((NB, 2 * DEPTH, 128), BF),
            vmem((128, 2 * DEPTH), BF),
            vmem((LAST, 3, 128, 512), BF),
            vmem((LAST, 3, 128, 512), BF),
            vmem((LAST, 128, 512), F32),
            vmem((LAST, 128, 256), F32),
            vmem((LAST, 128, 256), F32),
            vmem((NB, 128, 256), F32),
            vmem((8, 208, 128), jnp.int16),
            vmem((NB, 128, 128), F32),
            vmem((NB // 2, 2, DEPTH, 128), BF),
            vmem((8, 208, 128), jnp.int16),
            vmem((DEPTH,), jnp.int32),
            pltpu.SMEM((10,), F32),
            vmem((NB, 2, DEPTH, 128), BF),
            vmem((8, 128, 256), F32),
            vmem((8, 32, 256), BF),
            vmem((8, 32, 256), BF),
            vmem((7, 128, 256), BF),
            vmem((7, 128, 256), BF),
            dma((3,)),
            dma, dma, dma, dma,
            dma((NB, 2)), dma((NB, 2)),
            dma((LAST, 3)), dma((LAST, 3)),
            dma((LAST,)), dma((LAST,)),
            dma((NB,)), dma((NB,)),
            dma((8,)), dma((8,)),
            dma((NB // 2, 2)), dma((NB // 2, 2)),
            dma((7,)), dma((7,)),
            dma((8, 2)), dma((8, 2)),
        ],
        compiler_params=pltpu.CompilerParams(
            collective_id=0, has_side_effects=True, vmem_limit_bytes=50 * 2**20
        ),
        cost_estimate=pl.CostEstimate(flops=4 * 1536 * 2048 * 1024, bytes_accessed=8 * 2**20, transcendentals=0),
    )(*(pltpu.with_memory_space_constraint(a, pltpu.HBM) for a in (design, species, species_weight)))


def solution(mesh):
    placed = (P("row", "col"), P("row"), P())
    return jax.shard_map(
        shards, mesh=mesh, in_specs=placed, out_specs=P(("col", "row"), None), check_vma=False
    )
```
